32 devices in a mesh: grp: 4 (over y, x), cell: 8 (over z, core).
Axes of the slice: x: 2, y: 2, z: 4, core: 2. Of those that a mesh axis runs over, the one named last changes fastest.
Arguments:
- occurrence: bfloat16 [98304, 4096], P(('grp', 'cell')), may hold values from 0 to 1, as said below
- condition: bfloat16 [98304], P(('grp', 'cell')), may hold values from 0.05 to 1, as said below
- neighbours: int32 [768, 4], P(('grp', 'cell')), may hold values from 0 to 767, as said below
- pair_count: int32 [768], P(('grp', 'cell')), may hold values from 0 to 4
Outputs:
- effective: float32 [98304], P(('grp', 'cell'))
- persistence: float32 [4096], P(('grp', 'cell'))
The draws below stay inside these ranges and needn't reach their ends.
Inputs may be any that keep to these rules, and one draw needn't show every extreme that they name: occurrence probabilities, positive. habitat condition, positive. `neighbours`: entry k of row t, for k < pair_count[t], is a tile u != t with |u - t| <= 2 in the same band of 192 consecutive tiles (t // 192 == u // 192); entries are distinct; pairing is symmetric (u lists t whenever t lists u); later entries hold t.
All inputs are finite; a program needn't handle non-finite values.
Results may differ from the reference program's by a relative error of at most 0.0003.
Values may be sent and summed in bfloat16 or wider, within the bound.
A program may use at most 384 MiB of HBM per device.

```python
import jax
import jax.numpy as jnp
from jax import lax

SPECIES = 4096
TILE = 128
RADIUS = 2
TILES_DEV = 24
GROUP_TILES = 192
TILES = 768
CELLS = 98304


def draw_occurrence(key, part):
    first, second, third, fourth = jax.random.split(key, 4)
    tile_of = jnp.arange(CELLS, dtype=jnp.int32) // TILE
    range_start = jax.random.randint(third, (SPECIES,), 0, TILES).astype(jnp.int32)
    range_span = (jax.random.randint(fourth, (SPECIES,), 1, 9) * TILES_DEV).astype(jnp.int32)
    inside = jnp.mod(tile_of[:, None] - range_start[None, :], TILES) < range_span[None, :]
    boost = jnp.where(inside, 7.0, 0.0)
    noise = jax.random.normal(first, (CELLS, SPECIES), jnp.float32) * 1.5
    richness = jax.random.uniform(second, (CELLS, 1), jnp.float32, -0.5, 0.5)
    logits = -6.0 + noise + richness + boost
    return jax.nn.sigmoid(logits).astype(jnp.bfloat16)


def draw_condition(key, part):
    first, second = jax.random.split(key, 2)
    regions = TILES // TILES_DEV
    level = jnp.exp(jax.random.uniform(first, (regions,), jnp.float32, -2.0, 0.0))
    rough = jnp.exp(jax.random.uniform(second, (CELLS,), jnp.float32, -0.7, 0.0))
    level_cells = jnp.repeat(level, TILES_DEV * TILE)
    return (level_cells * rough).astype(jnp.bfloat16)


def pair_lists(key):
    folded = jax.random.fold_in(key, 17)
    coins = jax.random.randint(folded, (TILES, RADIUS), 0, 2).astype(jnp.int32)
    own_tiles = jnp.arange(TILES, dtype=jnp.int32)
    position = own_tiles % GROUP_TILES
    coins = jnp.where(position[:, None] < 2 * RADIUS, 1, coins)
    steps_up = jnp.arange(1, RADIUS + 1, dtype=jnp.int32)
    upward = (coins == 1) & (position[:, None] + steps_up[None, :] < GROUP_TILES)
    downward = []
    for offset in range(RADIUS, 0, -1):
        moved = jnp.roll(upward[:, offset - 1], offset)
        downward.append(moved & (position >= offset))
    valid = jnp.concatenate([jnp.stack(downward, 1), upward], 1)
    candidate = jnp.concatenate([own_tiles[:, None] - steps_up[::-1][None, :], own_tiles[:, None] + steps_up[None, :]], 1)
    candidate = jnp.where(valid, candidate, own_tiles[:, None])
    slot_ids = jnp.arange(2 * RADIUS, dtype=jnp.int32)[None, :]
    ranking = jnp.where(valid, slot_ids, slot_ids + 2 * RADIUS)
    ordering = jnp.argsort(ranking, axis=1, stable=True)
    lists = jnp.take_along_axis(candidate, ordering, axis=1)
    counts = jnp.sum(valid.astype(jnp.int32), axis=1)
    return (lists.astype(jnp.int32), counts.astype(jnp.int32))


def draw_neighbours(key, part):
    return pair_lists(key)[0]


def draw_pair_count(key, part):
    return pair_lists(key)[1]


def setup_inputs(seed: int = 0) -> dict:
    streams_of = jax.random.split(jax.random.key(seed), 5)
    occurrence = draw_occurrence(jax.random.fold_in(streams_of[4], 71), 0)
    condition = draw_condition(jax.random.fold_in(streams_of[4], 71), 0)
    neighbours = draw_neighbours(jax.random.fold_in(streams_of[4], 71), 0)
    pair_count = draw_pair_count(jax.random.fold_in(streams_of[4], 71), 0)
    return {"occurrence": occurrence, "condition": condition, "neighbours": neighbours, "pair_count": pair_count}


sharpness = 40.0
epsilon = 1e-06
exponent = 0.25

def pair_hits(neighbours, counts, first_tile, radius):
    own_tiles = first_tile + jnp.arange(counts.shape[0], dtype=jnp.int32)
    live_slot = jnp.arange(neighbours.shape[1], dtype=jnp.int32)[None, :] < counts[:, None]
    offsets = jnp.arange(-radius, radius + 1, dtype=jnp.int32)
    hit_tile = (neighbours - own_tiles[:, None])[:, :, None] == offsets[None, None, :]
    matched = jnp.any(live_slot[:, :, None] & hit_tile, axis=1) | (offsets == 0)[None, :]
    return matched.astype(jnp.float32)

def band_weights(row_block, window, row_inv, win_inv, hits_rows, shift, lowest, radius):
    per_block = hits_rows.shape[0]
    col_tiles = window.shape[0] // TILE
    gram_block = lax.dot_general(row_block, window, (((1,), (1,)), ((), ())), preferred_element_type=jnp.float32)
    cosine = gram_block * row_inv[:, None] * win_inv[None, :]
    distance = jnp.arange(col_tiles, dtype=jnp.int32)[None, :] - shift - jnp.arange(per_block, dtype=jnp.int32)[:, None]
    inside = (distance >= lowest) & (distance <= radius)
    picked = jnp.take_along_axis(hits_rows, jnp.clip(distance + radius, 0, 2 * radius), axis=1)
    tiles_mask = jnp.where(inside, picked, 0.0)
    diagonal = jnp.eye(TILE, dtype=bool)
    selfpair = (distance == 0)[:, None, :, None] & diagonal[None, :, None, :]
    spread = jnp.broadcast_to(tiles_mask[:, None, :, None], (per_block, TILE, col_tiles, TILE))
    cellmask = jnp.where(selfpair, 0.0, spread).reshape(per_block * TILE, col_tiles * TILE)
    return jnp.exp(sharpness * cosine) * cellmask

def inverse_norms(block_rows):
    wide = block_rows.astype(jnp.float32)
    return lax.rsqrt(lax.optimization_barrier(jnp.sum(wide * wide, axis=1)) + epsilon)

def reference(occurrence, condition, neighbours, pair_count):
    hits = pair_hits(neighbours, pair_count, 0, RADIUS)
    per_block = 4
    margin = jnp.zeros((RADIUS * TILE, SPECIES), occurrence.dtype)
    padded = jnp.concatenate([margin, occurrence, margin], 0)
    cond_full = condition.astype(jnp.float32)
    cond_margin = jnp.zeros((RADIUS * TILE,), jnp.float32)
    cond_pad = jnp.concatenate([cond_margin, cond_full, cond_margin], 0)
    width = (per_block + 2 * RADIUS) * TILE

    def one_block(block_id):
        start = block_id * (per_block * TILE)
        row_block = lax.dynamic_slice_in_dim(occurrence, start, per_block * TILE, 0)
        window = lax.dynamic_slice_in_dim(padded, start, width, 0)
        cond_win = lax.dynamic_slice_in_dim(cond_pad, start, width, 0)
        cond_rows = lax.dynamic_slice_in_dim(cond_full, start, per_block * TILE, 0)
        hits_rows = lax.dynamic_slice_in_dim(hits, block_id * per_block, per_block, 0)
        weights = band_weights(row_block, window, inverse_norms(row_block), inverse_norms(window), hits_rows, RADIUS, -RADIUS, RADIUS)
        numer = lax.optimization_barrier(jnp.sum(weights * cond_win[None, :], axis=1))
        denom = lax.optimization_barrier(jnp.sum(weights, axis=1))
        return cond_rows * numer / denom
    effective = lax.map(one_block, jnp.arange(TILES // per_block, dtype=jnp.int32)).reshape(CELLS)
    weighted = jnp.stack([effective.astype(jnp.bfloat16), jnp.ones((CELLS,), jnp.float32).astype(jnp.bfloat16)])
    totals = jnp.dot(weighted, occurrence, preferred_element_type=jnp.float32)
    persistence = (totals[0] / totals[1]) ** exponent
    return (effective, persistence)
```

```python
import functools
import math

import jax
import jax.numpy as jnp
from jax import lax
from jax.experimental import pallas as pl
from jax.experimental.pallas import tpu as pltpu
from jax.sharding import PartitionSpec as P

sharpness = 40.0
epsilon = 1e-06

TILE = 128
PAIR = 2 * TILE
SCALE = sharpness * math.log2(math.e)


def gram_dot(a, b):
    return lax.dot_general(a, b, (((1,), (1,)), ((), ())), preferred_element_type=jnp.float32)


def fold_rows(x):
    return jnp.sum(x.reshape(x.shape[0] // 8, 8, x.shape[1]), axis=0)


def doubling(reach):
    steps = []
    d = 1
    while d < reach:
        steps.append(d)
        d *= 2
    return steps


def main_kernel(
    n_grp, n_cell, tiles, per, wide, occ_hbm, cond_ref, nb_ref, cnt_ref, eff_ref, tot_ref,
    own, halo, gram, irow, icol, crow, ccol, acc, xin, wl, sums, got,
    load_sem, halo_send, halo_recv, cond_send, cond_recv, acc_send, acc_recv,
    sum_send, sum_recv, from_left, from_right, from_before, from_after,
):
    rows = tiles * TILE
    pairs = tiles // 2
    species = own.shape[1]
    devices = n_grp * n_cell
    grp = lax.axis_index("grp")
    me = lax.axis_index("cell")
    rank = grp * n_cell + me
    first_tile = rank * tiles
    has_left = me > 0
    has_right = me < n_cell - 1
    left = (grp, jnp.maximum(me - 1, 0))
    right = (grp, jnp.minimum(me + 1, n_cell - 1))
    mesh_id = pl.DeviceIdType.MESH

    def load(k):
        start = k * PAIR if isinstance(k, int) else pl.multiple_of(k * PAIR, PAIR)
        return pltpu.make_async_copy(
            occ_hbm.at[pl.ds(start, PAIR)], own.at[pl.ds(start, PAIR)], load_sem.at[k]
        )

    barrier = pltpu.get_barrier_semaphore()

    @pl.when(has_left)
    def _():
        pl.semaphore_signal(barrier, inc=1, device_id=left, device_id_type=mesh_id)

    @pl.when(has_right)
    def _():
        pl.semaphore_signal(barrier, inc=1, device_id=right, device_id_type=mesh_id)

    for shift in (1, n_grp - 1):
        pl.semaphore_signal(
            barrier, inc=1, device_id=(lax.rem(grp + shift, n_grp), me), device_id_type=mesh_id
        )

    for k in range(pairs):
        load(k).start()

    cond = cond_ref[...].astype(jnp.float32)
    for t in range(tiles):
        crow[t + 1] = jnp.broadcast_to(cond[t : t + 1, :], (8, TILE))

    pl.semaphore_wait(barrier, has_left.astype(jnp.int32) + has_right.astype(jnp.int32) + 2)

    def remote(src, dst, send, recv, slot, target):
        return pltpu.make_async_remote_copy(
            src_ref=src, dst_ref=dst, send_sem=send.at[slot], recv_sem=recv.at[slot],
            device_id=target, device_id_type=mesh_id,
        )

    halo_r = remote(
        occ_hbm.at[pl.ds(rows - TILE, TILE)], halo.at[0], halo_send, halo_recv, 0, right
    )
    halo_l = remote(occ_hbm.at[pl.ds(0, TILE)], halo.at[1], halo_send, halo_recv, 1, left)
    cond_r = remote(crow.at[tiles], crow.at[0], cond_send, cond_recv, 0, right)
    cond_l = remote(crow.at[1], crow.at[tiles + 1], cond_send, cond_recv, 1, left)
    acc_r = remote(acc.at[tiles + 1], xin.at[0], acc_send, acc_recv, 0, right)
    acc_l = remote(acc.at[0], xin.at[1], acc_send, acc_recv, 1, left)

    @pl.when(has_right)
    def _():
        halo_r.start()
        cond_r.start()

    @pl.when(has_left)
    def _():
        halo_l.start()
        cond_l.start()

    @pl.when(jnp.logical_not(has_left))
    def _():
        halo[0] = jnp.zeros((TILE, species), halo.dtype)
        crow[0] = jnp.zeros((8, TILE), jnp.float32)
        xin[0] = jnp.zeros((16, TILE), jnp.float32)

    @pl.when(jnp.logical_not(has_right))
    def _():
        halo[1] = jnp.zeros((TILE, species), halo.dtype)
        crow[tiles + 1] = jnp.zeros((8, TILE), jnp.float32)
        xin[1] = jnp.zeros((16, TILE), jnp.float32)

    def grp_round(r, d):
        for shift, sem in ((d, from_before), (n_grp - d, from_after)):
            pl.semaphore_signal(
                sem.at[r], inc=1, device_id=(lax.rem(grp + shift, n_grp), me), device_id_type=mesh_id
            )
        pl.semaphore_wait(from_before.at[r], 1)
        pl.semaphore_wait(from_after.at[r], 1)

    def cell_round(r, d):
        low = me >= d
        high = me + d < n_cell

        @pl.when(low)
        def _():
            pl.semaphore_signal(
                from_right.at[r], inc=1, device_id=(grp, jnp.maximum(me - d, 0)),
                device_id_type=mesh_id,
            )

        @pl.when(high)
        def _():
            pl.semaphore_signal(
                from_left.at[r], inc=1, device_id=(grp, jnp.minimum(me + d, n_cell - 1)),
                device_id_type=mesh_id,
            )

        @pl.when(low)
        def _():
            pl.semaphore_wait(from_left.at[r], 1)

        @pl.when(high)
        def _():
            pl.semaphore_wait(from_right.at[r], 1)

    rounds = [
        functools.partial(grp_round, r, d) for r, d in enumerate(doubling((n_grp + 1) // 2))
    ]
    rounds += [functools.partial(cell_round, r, d) for r, d in enumerate(doubling(n_cell))]

    def column(row8):
        return jnp.transpose(jnp.broadcast_to(row8[0:1, :], (TILE, TILE)))

    for e in range(1, tiles + 1):
        ccol[e] = column(crow[e])

    def hit(t, offset):
        wanted = first_tile + t + offset
        found = jnp.int32(0)
        for s in range(nb_ref.shape[0]):
            same = jnp.logical_and(nb_ref[s, t] == wanted, s < cnt_ref[t])
            found = jnp.maximum(found, same.astype(jnp.int32))
        return found.astype(jnp.float32)

    eye = lax.broadcasted_iota(jnp.int32, (TILE, TILE), 0) == lax.broadcasted_iota(
        jnp.int32, (TILE, TILE), 1
    )

    def part(slot, base, i, j):
        return gram[slot, base + i * TILE : base + (i + 1) * TILE, j * TILE : (j + 1) * TILE]

    def own_own(slot, base, k):
        e = 2 * k + 1
        near = hit(2 * k, 1)
        tiles_g = [[part(slot, base, i, j) for j in range(2)] for i in range(2)]
        rows_inv = []
        cols_inv = []
        for i in range(2):
            diag = jnp.sum(jnp.where(eye, tiles_g[i][i], 0.0), axis=0, keepdims=True)
            inv = jnp.broadcast_to(lax.rsqrt(diag + epsilon), (TILE, TILE))
            col = jnp.transpose(inv) * SCALE
            irow[e + i] = inv[0:8]
            icol[e + i] = col
            rows_inv.append(inv[0:1])
            cols_inv.append(col)
        cc = [ccol[e], ccol[e + 1]]
        w = [[None, None], [None, None]]
        for i in range(2):
            for j in range(2):
                v = jnp.exp2(tiles_g[i][j] * cols_inv[i] * rows_inv[j])
                w[i][j] = jnp.where(eye, 0.0, v) if i == j else v * near
        for j in range(2):
            acc[e + j, 0:8, :] = fold_rows(w[0][j] * cc[0] + w[1][j] * cc[1])
            acc[e + j, 8:16, :] = fold_rows(w[0][j] + w[1][j])

    def prev_own(slot, k):
        e = 2 * k + 1
        far0, near1, far1 = hit(2 * k - 2, 2), hit(2 * k - 1, 1), hit(2 * k - 1, 2)
        r0, r1 = irow[e, 0:1, :], irow[e + 1, 0:1, :]
        w00 = jnp.exp2(part(slot, 0, 0, 0) * icol[e - 2] * r0) * far0
        w10 = jnp.exp2(part(slot, 0, 1, 0) * icol[e - 1] * r0) * near1
        w11 = jnp.exp2(part(slot, 0, 1, 1) * icol[e - 1] * r1) * far1
        cp0, cp1 = ccol[e - 2], ccol[e - 1]
        acc[e, 0:8, :] += fold_rows(w00 * cp0 + w10 * cp1)
        acc[e, 8:16, :] += fold_rows(w00 + w10)
        acc[e + 1, 0:8, :] += fold_rows(w11 * cp1)
        acc[e + 1, 8:16, :] += fold_rows(w11)
        c0, c1 = crow[e, 0:1, :], crow[e + 1, 0:1, :]
        acc[e - 2, 0:8, :] += fold_rows(jnp.transpose(w00 * c0))
        acc[e - 2, 8:16, :] += fold_rows(jnp.transpose(w00))
        acc[e - 1, 0:8, :] += fold_rows(jnp.transpose(w10 * c0 + w11 * c1))
        acc[e - 1, 8:16, :] += fold_rows(jnp.transpose(w10 + w11))

    def pair_rows(k, count=1):
        start = k * PAIR if isinstance(k, int) else pl.multiple_of(k * PAIR, PAIR)
        return own[pl.ds(start, count * PAIR), :]

    def block(k, slot):
        gram[slot] = gram_dot(pair_rows(k - 1, 2), pair_rows(k))

    load(0).wait()
    gram[0, PAIR:, :] = gram_dot(pair_rows(0), pair_rows(0))
    load(1).wait()
    block(1, 1)
    own_own(0, PAIR, 0)

    def step(i, carry):
        k = i + 2
        slot = lax.rem(k, 2)
        load(k).wait()
        block(k, slot)
        own_own(1 - slot, PAIR, k - 1)
        prev_own(1 - slot, k - 1)
        for r, one in enumerate(rounds):
            pl.when(i == min(r + 1, pairs - 3))(one)
        return carry

    lax.fori_loop(0, pairs - 2, step, 0)
    slot = (pairs - 1) % 2
    own_own(slot, PAIR, pairs - 1)
    prev_own(slot, pairs - 1)

    @pl.when(has_left)
    def _():
        halo_r.wait_recv()
        cond_r.wait_recv()

    @pl.when(has_right)
    def _():
        halo_l.wait_recv()
        cond_l.wait_recv()

    ccol[0] = column(crow[0])
    ccol[tiles + 1] = column(crow[tiles + 1])

    def halo_inverse(side):
        total = jnp.zeros((TILE, TILE), jnp.float32)
        for q in range(species // TILE):
            x = halo[side, :, q * TILE : (q + 1) * TILE].astype(jnp.float32)
            total = total + x * x
        return lax.rsqrt(jnp.sum(total, axis=1, keepdims=True) + epsilon) * SCALE

    edge_l = gram_dot(halo[0], pair_rows(0))
    edge_r = gram_dot(halo[1], own[rows - PAIR : rows - TILE, :])
    inv_l = jnp.broadcast_to(halo_inverse(0), (TILE, TILE))
    inv_r = jnp.broadcast_to(halo_inverse(1), (TILE, TILE))
    w0 = jnp.exp2(edge_l[:, 0:TILE] * inv_l * irow[1, 0:1, :]) * hit(0, -1)
    w1 = jnp.exp2(edge_l[:, TILE:] * inv_l * irow[2, 0:1, :]) * hit(1, -2)
    acc[0, 0:8, :] = fold_rows(jnp.transpose(w0 * crow[1, 0:1, :] + w1 * crow[2, 0:1, :]))
    acc[0, 8:16, :] = fold_rows(jnp.transpose(w0 + w1))
    w2 = jnp.exp2(edge_r * inv_r * irow[tiles - 1, 0:1, :]) * hit(tiles - 2, 2)
    acc[tiles + 1, 0:8, :] = fold_rows(jnp.transpose(w2 * crow[tiles - 1, 0:1, :]))
    acc[tiles + 1, 8:16, :] = fold_rows(jnp.transpose(w2))

    @pl.when(has_right)
    def _():
        acc_r.start()

    @pl.when(has_left)
    def _():
        acc_l.start()

    acc[1, 0:8, :] += fold_rows(w0 * ccol[0])
    acc[1, 8:16, :] += fold_rows(w0)
    acc[2, 0:8, :] += fold_rows(w1 * ccol[0])
    acc[2, 8:16, :] += fold_rows(w1)
    acc[tiles - 1, 0:8, :] += fold_rows(w2 * ccol[tiles + 1])
    acc[tiles - 1, 8:16, :] += fold_rows(w2)

    line = lax.broadcasted_iota(jnp.int32, (16, TILE), 0)

    def finish(t, extra=None):
        e = t + 1
        total = acc[e]
        if extra is not None:
            total = total + xin[extra]
        numer = jnp.sum(total[0:8], axis=0, keepdims=True)
        denom = jnp.sum(total[8:16], axis=0, keepdims=True)
        eff = crow[e, 0:1, :] * numer / denom
        eff_ref[t : t + 1, :] = eff
        both = jnp.where(line == 0, eff, jnp.where(line == 1, 1.0, 0.0))
        wl[:, t * TILE : (t + 1) * TILE] = both.astype(jnp.bfloat16)

    for t in range(1, tiles - 1):
        finish(t)

    wide_step = 512 if species % 512 == 0 else TILE
    blocks = wide_step // TILE

    def inner(i, carry):
        cols = pl.ds(pl.multiple_of(i * wide_step, wide_step), wide_step)
        value = jnp.dot(
            wl[:, PAIR : rows - PAIR], own[PAIR : rows - PAIR, cols],
            preferred_element_type=jnp.float32,
        )
        for q in range(blocks):
            sums[i * blocks + q] = value[0:2, q * TILE : (q + 1) * TILE]
        return carry

    lax.fori_loop(0, species // wide_step, inner, 0)

    @pl.when(has_left)
    def _():
        acc_r.wait_recv()

    @pl.when(has_right)
    def _():
        acc_l.wait_recv()

    finish(0, 0)
    finish(tiles - 1, 1)

    def outer(i, carry):
        cols = pl.ds(pl.multiple_of(i * wide_step, wide_step), wide_step)
        value = jnp.dot(
            wl[:, 0:PAIR], own[0:PAIR, cols], preferred_element_type=jnp.float32
        ) + jnp.dot(
            wl[:, rows - PAIR : rows], own[rows - PAIR : rows, cols],
            preferred_element_type=jnp.float32,
        )
        for q in range(blocks):
            sums[i * blocks + q] += value[0:2, q * TILE : (q + 1) * TILE]
        return carry

    lax.fori_loop(0, species // wide_step, outer, 0)

    def send(j, carry):
        owner = lax.rem(rank + j, devices)
        pltpu.make_async_remote_copy(
            src_ref=sums.at[owner * per // wide], dst_ref=got.at[j], send_sem=sum_send,
            recv_sem=sum_recv, device_id=(owner // n_cell, lax.rem(owner, n_cell)),
            device_id_type=mesh_id,
        ).start()
        return carry

    lax.fori_loop(1, devices, send, 0)
    got[0] = sums[rank * per // wide]
    others = got.at[pl.ds(1, devices - 1)]
    pltpu.make_async_copy(others, others, sum_recv).wait()
    tot_ref[...] = jnp.sum(got[...], axis=0)
    pltpu.make_async_copy(others, others, sum_send).wait()

    @pl.when(has_right)
    def _():
        halo_r.wait_send()
        cond_r.wait_send()
        acc_r.wait_send()

    @pl.when(has_left)
    def _():
        halo_l.wait_send()
        cond_l.wait_send()
        acc_l.wait_send()


def close_kernel(eff_ref, tot_ref, eff_out, per_out):
    eff_out[...] = eff_ref[...]
    per_out[...] = jnp.sqrt(jnp.sqrt(tot_ref[0:1, :] / tot_ref[1:2, :]))


def per_device(n_grp, n_cell, occurrence, condition, neighbours, pair_count):
    tiles = pair_count.shape[0]
    rows, species = occurrence.shape
    devices = n_grp * n_cell
    per = species // devices
    wide = max(per, TILE)
    vmem = pl.BlockSpec(memory_space=pltpu.VMEM)
    smem = pl.BlockSpec(memory_space=pltpu.SMEM)
    dma = pltpu.SemaphoreType.DMA
    cell_sems = pltpu.SemaphoreType.REGULAR((max(len(doubling(n_cell)), 1),))
    grp_sems = pltpu.SemaphoreType.REGULAR((max(len(doubling((n_grp + 1) // 2)), 1),))
    effective, totals = pl.pallas_call(
        functools.partial(main_kernel, n_grp, n_cell, tiles, per, wide),
        out_shape=(
            jax.ShapeDtypeStruct((tiles, TILE), jnp.float32),
            jax.ShapeDtypeStruct((2, wide), jnp.float32),
        ),
        in_specs=[pl.BlockSpec(memory_space=pl.ANY), vmem, smem, smem],
        out_specs=(vmem, vmem),
        scratch_shapes=[
            pltpu.VMEM((rows, species), jnp.bfloat16),
            pltpu.VMEM((2, TILE, species), jnp.bfloat16),
            pltpu.VMEM((2, 2 * PAIR, PAIR), jnp.float32),
            pltpu.VMEM((tiles + 2, 8, TILE), jnp.float32),
            pltpu.VMEM((tiles + 2, TILE, TILE), jnp.float32),
            pltpu.VMEM((tiles + 2, 8, TILE), jnp.float32),
            pltpu.VMEM((tiles + 2, TILE, TILE), jnp.float32),
            pltpu.VMEM((tiles + 2, 16, TILE), jnp.float32),
            pltpu.VMEM((2, 16, TILE), jnp.float32),
            pltpu.VMEM((16, rows), jnp.bfloat16),
            pltpu.VMEM((species // wide, 2, wide), jnp.float32),
            pltpu.VMEM((devices, 2, wide), jnp.float32),
            dma((tiles // 2,)), dma((2,)), dma((2,)), dma((2,)), dma((2,)), dma((2,)), dma((2,)),
            dma, dma, cell_sems, cell_sems, grp_sems, grp_sems,
        ],
        compiler_params=pltpu.CompilerParams(
            collective_id=0, has_side_effects=True, vmem_limit_bytes=56 * 2**20
        ),
    )(occurrence, condition.reshape(tiles, TILE), neighbours.T, pair_count)
    effective, persistence = pl.pallas_call(
        close_kernel,
        out_shape=(
            jax.ShapeDtypeStruct((tiles, TILE), jnp.float32),
            jax.ShapeDtypeStruct((1, wide), jnp.float32),
        ),
        in_specs=[vmem, vmem],
        out_specs=(vmem, vmem),
    )(effective, totals)
    persistence = persistence.reshape(wide)
    if per < wide:
        offset = lax.rem(lax.axis_index(("grp", "cell")) * per, wide)
        persistence = lax.dynamic_slice_in_dim(persistence, offset, per)
    return effective.reshape(rows), persistence


def solution(mesh):
    return jax.shard_map(
        functools.partial(per_device, mesh.shape["grp"], mesh.shape["cell"]),
        mesh=mesh,
        in_specs=(
            P(("grp", "cell"), None),
            P(("grp", "cell")),
            P(("grp", "cell"), None),
            P(("grp", "cell")),
        ),
        out_specs=(P(("grp", "cell")), P(("grp", "cell"))),
        check_vma=False,
    )
```

```python
import functools
import math

import jax
import jax.numpy as jnp
from jax import lax
from jax.experimental import pallas as pl
from jax.experimental.pallas import tpu as pltpu
from jax.sharding import PartitionSpec as P

sharpness = 40.0
epsilon = 1e-06

TILE = 128
PAIR = 2 * TILE
GROUP = 2
SCALE = sharpness * math.log2(math.e)


def gram_dot(a, b):
    return lax.dot_general(a, b, (((1,), (1,)), ((), ())), preferred_element_type=jnp.float32)


def fold_rows(x):
    return jnp.sum(x.reshape(x.shape[0] // 8, 8, x.shape[1]), axis=0)


def main_kernel(
    n_grp, n_cell, tiles, per, wide, occ_hbm, cond_ref, nb_ref, cnt_ref, eff_ref, tot_ref,
    own, halo, gram, irow, icol, crow, ccol, acc, xin, wl, sums, got,
    load_sem, halo_send, halo_recv, cond_send, cond_recv, acc_send, acc_recv,
    sum_send, sum_recv,
):
    rows = tiles * TILE
    pairs = tiles // 2
    species = own.shape[1]
    devices = n_grp * n_cell
    grp = lax.axis_index("grp")
    me = lax.axis_index("cell")
    rank = grp * n_cell + me
    first_tile = rank * tiles
    has_left = me > 0
    has_right = me < n_cell - 1
    left = (grp, jnp.maximum(me - 1, 0))
    right = (grp, jnp.minimum(me + 1, n_cell - 1))
    mesh_id = pl.DeviceIdType.MESH

    def load(k):
        start = k * PAIR if isinstance(k, int) else pl.multiple_of(k * PAIR, PAIR)
        return pltpu.make_async_copy(
            occ_hbm.at[pl.ds(start, PAIR)], own.at[pl.ds(start, PAIR)], load_sem.at[k]
        )

    barrier = pltpu.get_barrier_semaphore()

    for k in range(2):
        load(k).start()

    def greet(j, carry):
        other = lax.rem(rank + j, devices)
        pl.semaphore_signal(
            barrier, inc=1, device_id=(other // n_cell, lax.rem(other, n_cell)),
            device_id_type=mesh_id,
        )
        return carry

    lax.fori_loop(1, devices, greet, 0, unroll=True)

    for k in range(2, pairs):
        load(k).start()

    cond = cond_ref[...].astype(jnp.float32)
    for t in range(tiles):
        crow[t + 1] = jnp.broadcast_to(cond[t : t + 1, :], (8, TILE))

    def remote(src, dst, send, recv, slot, target):
        return pltpu.make_async_remote_copy(
            src_ref=src, dst_ref=dst, send_sem=send.at[slot], recv_sem=recv.at[slot],
            device_id=target, device_id_type=mesh_id,
        )

    halo_r = remote(
        occ_hbm.at[pl.ds(rows - TILE, TILE)], halo.at[0], halo_send, halo_recv, 0, right
    )
    halo_l = remote(occ_hbm.at[pl.ds(0, TILE)], halo.at[1], halo_send, halo_recv, 1, left)
    cond_r = remote(crow.at[tiles], crow.at[0], cond_send, cond_recv, 0, right)
    cond_l = remote(crow.at[1], crow.at[tiles + 1], cond_send, cond_recv, 1, left)
    acc_r = remote(acc.at[tiles + 1], xin.at[0], acc_send, acc_recv, 0, right)
    acc_l = remote(acc.at[0], xin.at[1], acc_send, acc_recv, 1, left)

    def column(row8):
        return jnp.transpose(jnp.broadcast_to(row8[0:1, :], (TILE, TILE)))

    def hit(t, offset):
        wanted = first_tile + t + offset
        found = jnp.int32(0)
        for s in range(nb_ref.shape[0]):
            same = jnp.logical_and(nb_ref[s, t] == wanted, s < cnt_ref[t])
            found = jnp.maximum(found, same.astype(jnp.int32))
        return found.astype(jnp.float32)

    eye = lax.broadcasted_iota(jnp.int32, (TILE, TILE), 0) == lax.broadcasted_iota(
        jnp.int32, (TILE, TILE), 1
    )

    def part(slot, base, i, j):
        return gram[slot, base + i * TILE : base + (i + 1) * TILE, j * TILE : (j + 1) * TILE]

    def own_own(slot, base, k):
        e = 2 * k + 1
        near = hit(2 * k, 1)
        tiles_g = [[part(slot, base, i, j) for j in range(2)] for i in range(2)]
        rows_inv = []
        cols_inv = []
        for i in range(2):
            diag = jnp.sum(jnp.where(eye, tiles_g[i][i], 0.0), axis=0, keepdims=True)
            inv = jnp.broadcast_to(lax.rsqrt(diag + epsilon), (TILE, TILE))
            col = jnp.transpose(inv) * SCALE
            irow[e + i] = inv[0:8]
            icol[e + i] = col
            rows_inv.append(inv[0:1])
            cols_inv.append(col)
        cc = [column(crow[e]), column(crow[e + 1])]
        ccol[e] = cc[0]
        ccol[e + 1] = cc[1]
        w = [[None, None], [None, None]]
        for i in range(2):
            for j in range(2):
                v = jnp.exp2(tiles_g[i][j] * cols_inv[i] * rows_inv[j])
                w[i][j] = jnp.where(eye, 0.0, v) if i == j else v * near
        for j in range(2):
            acc[e + j, 0:8, :] = fold_rows(w[0][j] * cc[0] + w[1][j] * cc[1])
            acc[e + j, 8:16, :] = fold_rows(w[0][j] + w[1][j])

    def prev_own(slot, k):
        e = 2 * k + 1
        far0, near1, far1 = hit(2 * k - 2, 2), hit(2 * k - 1, 1), hit(2 * k - 1, 2)
        r0, r1 = irow[e, 0:1, :], irow[e + 1, 0:1, :]
        w00 = jnp.exp2(part(slot, 0, 0, 0) * icol[e - 2] * r0) * far0
        w10 = jnp.exp2(part(slot, 0, 1, 0) * icol[e - 1] * r0) * near1
        w11 = jnp.exp2(part(slot, 0, 1, 1) * icol[e - 1] * r1) * far1
        cp0, cp1 = ccol[e - 2], ccol[e - 1]
        acc[e, 0:8, :] += fold_rows(w00 * cp0 + w10 * cp1)
        acc[e, 8:16, :] += fold_rows(w00 + w10)
        acc[e + 1, 0:8, :] += fold_rows(w11 * cp1)
        acc[e + 1, 8:16, :] += fold_rows(w11)
        c0, c1 = crow[e, 0:1, :], crow[e + 1, 0:1, :]
        acc[e - 2, 0:8, :] += fold_rows(jnp.transpose(w00 * c0))
        acc[e - 2, 8:16, :] += fold_rows(jnp.transpose(w00))
        acc[e - 1, 0:8, :] += fold_rows(jnp.transpose(w10 * c0 + w11 * c1))
        acc[e - 1, 8:16, :] += fold_rows(jnp.transpose(w10 + w11))

    def pair_rows(k, count=1):
        start = k * PAIR if isinstance(k, int) else pl.multiple_of(k * PAIR, PAIR)
        return own[pl.ds(start, count * PAIR), :]

    def block(k, slot):
        gram[slot] = gram_dot(pair_rows(k - 1, 2), pair_rows(k))

    load(0).wait()
    gram[0, PAIR:, :] = gram_dot(pair_rows(0), pair_rows(0))
    pl.semaphore_wait(barrier, devices - 1)

    @pl.when(has_right)
    def _():
        halo_r.start()
        cond_r.start()

    @pl.when(has_left)
    def _():
        halo_l.start()
        cond_l.start()

    @pl.when(jnp.logical_not(has_left))
    def _():
        halo[0] = jnp.zeros((TILE, species), halo.dtype)
        crow[0] = jnp.zeros((8, TILE), jnp.float32)
        xin[0] = jnp.zeros((16, TILE), jnp.float32)

    @pl.when(jnp.logical_not(has_right))
    def _():
        halo[1] = jnp.zeros((TILE, species), halo.dtype)
        crow[tiles + 1] = jnp.zeros((8, TILE), jnp.float32)
        xin[1] = jnp.zeros((16, TILE), jnp.float32)

    load(1).wait()
    block(1, 1)
    own_own(0, PAIR, 0)

    def step(i, carry):
        first = 2 + GROUP * i
        for u in range(GROUP):
            load(first + u).wait()
        for u in range(GROUP):
            block(first + u, u % 2)
            own_own(1 - u % 2, PAIR, first + u - 1)
            prev_own(1 - u % 2, first + u - 1)
        return carry

    steps = (pairs - 2) // GROUP
    lax.fori_loop(0, steps, step, 0)
    for k in range(2 + GROUP * steps, pairs):
        load(k).wait()
        block(k, k % 2)
        own_own(1 - k % 2, PAIR, k - 1)
        prev_own(1 - k % 2, k - 1)
    slot = (pairs - 1) % 2
    own_own(slot, PAIR, pairs - 1)
    prev_own(slot, pairs - 1)

    @pl.when(has_left)
    def _():
        halo_r.wait_recv()
        cond_r.wait_recv()

    @pl.when(has_right)
    def _():
        halo_l.wait_recv()
        cond_l.wait_recv()

    ccol[0] = column(crow[0])
    ccol[tiles + 1] = column(crow[tiles + 1])

    def halo_inverse(side):
        total = jnp.zeros((TILE, TILE), jnp.float32)
        for q in range(species // TILE):
            x = halo[side, :, q * TILE : (q + 1) * TILE].astype(jnp.float32)
            total = total + x * x
        return lax.rsqrt(jnp.sum(total, axis=1, keepdims=True) + epsilon) * SCALE

    edge_l = gram_dot(halo[0], pair_rows(0))
    edge_r = gram_dot(halo[1], own[rows - PAIR : rows - TILE, :])
    inv_l = jnp.broadcast_to(halo_inverse(0), (TILE, TILE))
    inv_r = jnp.broadcast_to(halo_inverse(1), (TILE, TILE))
    w0 = jnp.exp2(edge_l[:, 0:TILE] * inv_l * irow[1, 0:1, :]) * hit(0, -1)
    w1 = jnp.exp2(edge_l[:, TILE:] * inv_l * irow[2, 0:1, :]) * hit(1, -2)
    acc[0, 0:8, :] = fold_rows(jnp.transpose(w0 * crow[1, 0:1, :] + w1 * crow[2, 0:1, :]))
    acc[0, 8:16, :] = fold_rows(jnp.transpose(w0 + w1))
    w2 = jnp.exp2(edge_r * inv_r * irow[tiles - 1, 0:1, :]) * hit(tiles - 2, 2)
    acc[tiles + 1, 0:8, :] = fold_rows(jnp.transpose(w2 * crow[tiles - 1, 0:1, :]))
    acc[tiles + 1, 8:16, :] = fold_rows(jnp.transpose(w2))

    @pl.when(has_right)
    def _():
        acc_r.start()

    @pl.when(has_left)
    def _():
        acc_l.start()

    acc[1, 0:8, :] += fold_rows(w0 * ccol[0])
    acc[1, 8:16, :] += fold_rows(w0)
    acc[2, 0:8, :] += fold_rows(w1 * ccol[0])
    acc[2, 8:16, :] += fold_rows(w1)
    acc[tiles - 1, 0:8, :] += fold_rows(w2 * ccol[tiles + 1])
    acc[tiles - 1, 8:16, :] += fold_rows(w2)

    line = lax.broadcasted_iota(jnp.int32, (16, TILE), 0)

    def finish(t, extra=None):
        e = t + 1
        total = acc[e]
        if extra is not None:
            total = total + xin[extra]
        numer = jnp.sum(total[0:8], axis=0, keepdims=True)
        denom = jnp.sum(total[8:16], axis=0, keepdims=True)
        eff = crow[e, 0:1, :] * numer / denom
        eff_ref[t : t + 1, :] = eff
        both = jnp.where(line == 0, eff, jnp.where(line == 1, 1.0, 0.0))
        wl[:, t * TILE : (t + 1) * TILE] = both.astype(jnp.bfloat16)

    for t in range(1, tiles - 1):
        finish(t)

    wide_step = 512 if species % 512 == 0 else TILE
    blocks = wide_step // TILE

    def inner(i, carry):
        cols = pl.ds(pl.multiple_of(i * wide_step, wide_step), wide_step)
        value = jnp.dot(
            wl[:, PAIR : rows - PAIR], own[PAIR : rows - PAIR, cols],
            preferred_element_type=jnp.float32,
        )
        for q in range(blocks):
            sums[i * blocks + q] = value[0:2, q * TILE : (q + 1) * TILE]
        return carry

    lax.fori_loop(0, species // wide_step, inner, 0)

    @pl.when(has_left)
    def _():
        acc_r.wait_recv()

    @pl.when(has_right)
    def _():
        acc_l.wait_recv()

    finish(0, 0)
    finish(tiles - 1, 1)

    share = wide // per

    def outer(i, carry):
        chunk = lax.rem(i + rank // (blocks * share), species // wide_step)
        cols = pl.ds(pl.multiple_of(chunk * wide_step, wide_step), wide_step)
        value = jnp.dot(
            wl[:, 0:PAIR], own[0:PAIR, cols], preferred_element_type=jnp.float32
        ) + jnp.dot(
            wl[:, rows - PAIR : rows], own[rows - PAIR : rows, cols],
            preferred_element_type=jnp.float32,
        )
        for q in range(blocks):
            sums[chunk * blocks + q] += value[0:2, q * TILE : (q + 1) * TILE]
        for q in range(blocks * share):
            owner = chunk * blocks * share + q

            @pl.when(owner != rank)
            def _():
                pltpu.make_async_remote_copy(
                    src_ref=sums.at[chunk * blocks + q // share],
                    dst_ref=got.at[lax.rem(rank - owner + devices, devices)],
                    send_sem=sum_send, recv_sem=sum_recv,
                    device_id=(owner // n_cell, lax.rem(owner, n_cell)), device_id_type=mesh_id,
                ).start()

        return carry

    lax.fori_loop(0, species // wide_step, outer, 0)
    got[0] = sums[rank // share]
    others = got.at[pl.ds(1, devices - 1)]
    pltpu.make_async_copy(others, others, sum_recv).wait()
    tot_ref[...] = jnp.sum(got[...], axis=0)
    pltpu.make_async_copy(others, others, sum_send).wait()

    @pl.when(has_right)
    def _():
        halo_r.wait_send()
        cond_r.wait_send()
        acc_r.wait_send()

    @pl.when(has_left)
    def _():
        halo_l.wait_send()
        cond_l.wait_send()
        acc_l.wait_send()


def close_kernel(eff_ref, tot_ref, eff_out, per_out):
    eff_out[...] = eff_ref[...]
    per_out[...] = jnp.sqrt(jnp.sqrt(tot_ref[0:1, :] / tot_ref[1:2, :]))


def per_device(n_grp, n_cell, occurrence, condition, neighbours, pair_count):
    tiles = pair_count.shape[0]
    rows, species = occurrence.shape
    devices = n_grp * n_cell
    per = species // devices
    wide = max(per, TILE)
    vmem = pl.BlockSpec(memory_space=pltpu.VMEM)
    smem = pl.BlockSpec(memory_space=pltpu.SMEM)
    dma = pltpu.SemaphoreType.DMA
    effective, totals = pl.pallas_call(
        functools.partial(main_kernel, n_grp, n_cell, tiles, per, wide),
        out_shape=(
            jax.ShapeDtypeStruct((tiles, TILE), jnp.float32),
            jax.ShapeDtypeStruct((2, wide), jnp.float32),
        ),
        in_specs=[pl.BlockSpec(memory_space=pl.ANY), vmem, smem, smem],
        out_specs=(vmem, vmem),
        scratch_shapes=[
            pltpu.VMEM((rows, species), jnp.bfloat16),
            pltpu.VMEM((2, TILE, species), jnp.bfloat16),
            pltpu.VMEM((2, 2 * PAIR, PAIR), jnp.float32),
            pltpu.VMEM((tiles + 2, 8, TILE), jnp.float32),
            pltpu.VMEM((tiles + 2, TILE, TILE), jnp.float32),
            pltpu.VMEM((tiles + 2, 8, TILE), jnp.float32),
            pltpu.VMEM((tiles + 2, TILE, TILE), jnp.float32),
            pltpu.VMEM((tiles + 2, 16, TILE), jnp.float32),
            pltpu.VMEM((2, 16, TILE), jnp.float32),
            pltpu.VMEM((16, rows), jnp.bfloat16),
            pltpu.VMEM((species // wide, 2, wide), jnp.float32),
            pltpu.VMEM((devices, 2, wide), jnp.float32),
            dma((tiles // 2,)), dma((2,)), dma((2,)), dma((2,)), dma((2,)), dma((2,)), dma((2,)),
            dma, dma,
        ],
        compiler_params=pltpu.CompilerParams(
            collective_id=0, has_side_effects=True, vmem_limit_bytes=56 * 2**20
        ),
    )(occurrence, condition.reshape(tiles, TILE), neighbours.T, pair_count)
    effective, persistence = pl.pallas_call(
        close_kernel,
        out_shape=(
            jax.ShapeDtypeStruct((tiles, TILE), jnp.float32),
            jax.ShapeDtypeStruct((1, wide), jnp.float32),
        ),
        in_specs=[vmem, vmem],
        out_specs=(vmem, vmem),
    )(effective, totals)
    persistence = persistence.reshape(wide)
    if per < wide:
        offset = lax.rem(lax.axis_index(("grp", "cell")) * per, wide)
        persistence = lax.dynamic_slice_in_dim(persistence, offset, per)
    return effective.reshape(rows), persistence


def solution(mesh):
    return jax.shard_map(
        functools.partial(per_device, mesh.shape["grp"], mesh.shape["cell"]),
        mesh=mesh,
        in_specs=(
            P(("grp", "cell"), None),
            P(("grp", "cell")),
            P(("grp", "cell"), None),
            P(("grp", "cell")),
        ),
        out_specs=(P(("grp", "cell")), P(("grp", "cell"))),
        check_vma=False,
    )
```

```python
import functools
import math

import jax
import jax.numpy as jnp
from jax import lax
from jax.experimental import pallas as pl
from jax.experimental.pallas import tpu as pltpu
from jax.sharding import PartitionSpec as P

sharpness = 40.0
epsilon = 1e-06

TILE = 128
PAIR = 2 * TILE
GROUP = 2
LEAD = 4
HALO_AT = 1
SCALE = sharpness * math.log2(math.e)


def gram_dot(a, b):
    return lax.dot_general(a, b, (((1,), (1,)), ((), ())), preferred_element_type=jnp.float32)


def fold_rows(x):
    return jnp.sum(x.reshape(x.shape[0] // 8, 8, x.shape[1]), axis=0)


def main_kernel(
    n_grp, n_cell, tiles, per, wide, occ_hbm, cond_hbm, nb_hbm, cnt_hbm, eff_hbm, per_hbm,
    cond_ref, nb_ref, cnt_ref, eff_ref, per_ref, small_sem,
    own, halo, gram, irow, icol, crow, ccol, chalo, acc, xin, xout, wl, sums, got,
    load_sem, halo_send, halo_recv, cond_send, cond_recv, acc_send, acc_recv,
    sum_send, sum_recv,
):
    rows = tiles * TILE
    pairs = tiles // 2
    species = own.shape[1]
    devices = n_grp * n_cell
    grp = lax.axis_index("grp")
    me = lax.axis_index("cell")
    rank = grp * n_cell + me
    first_tile = rank * tiles
    has_left = me > 0
    has_right = me < n_cell - 1
    left = (grp, jnp.maximum(me - 1, 0))
    right = (grp, jnp.minimum(me + 1, n_cell - 1))
    mesh_id = pl.DeviceIdType.MESH

    def load(k):
        start = k * PAIR if isinstance(k, int) else pl.multiple_of(k * PAIR, PAIR)
        return pltpu.make_async_copy(
            occ_hbm.at[pl.ds(start, PAIR)], own.at[pl.ds(start + PAIR, PAIR)], load_sem.at[k]
        )

    barrier = pltpu.get_barrier_semaphore()

    small = [
        pltpu.make_async_copy(cond_hbm, cond_ref, small_sem.at[0]),
        pltpu.make_async_copy(nb_hbm, nb_ref, small_sem.at[1]),
        pltpu.make_async_copy(cnt_hbm, cnt_ref, small_sem.at[2]),
    ]
    for copy in small:
        copy.start()
    for k in range(2):
        load(k).start()

    def greet(j, carry):
        other = lax.rem(rank + j, devices)
        pl.semaphore_signal(
            barrier, inc=1, device_id=(other // n_cell, lax.rem(other, n_cell)),
            device_id_type=mesh_id,
        )
        return carry

    lax.fori_loop(1, devices, greet, 0, unroll=True)

    for k in range(2, pairs):
        load(k).start()
    for copy in small:
        copy.wait()

    cond = cond_ref[...].astype(jnp.float32)
    for e in range(LEAD):
        crow[e] = jnp.zeros((8, TILE), jnp.float32)
    for t in range(tiles):
        crow[t + LEAD] = jnp.broadcast_to(cond[t : t + 1, :], (8, TILE))

    def remote(src, dst, send, recv, slot, target):
        return pltpu.make_async_remote_copy(
            src_ref=src, dst_ref=dst, send_sem=send.at[slot], recv_sem=recv.at[slot],
            device_id=target, device_id_type=mesh_id,
        )

    halo_r = remote(
        occ_hbm.at[pl.ds(rows - TILE, TILE)], halo.at[pl.ds(0, TILE)], halo_send, halo_recv, 0, right
    )
    halo_l = remote(
        occ_hbm.at[pl.ds(0, TILE)], halo.at[pl.ds(TILE, TILE)], halo_send, halo_recv, 1, left
    )
    last = LEAD + tiles - 1
    cond_r = remote(crow.at[last], chalo.at[0], cond_send, cond_recv, 0, right)
    cond_l = remote(crow.at[LEAD], chalo.at[1], cond_send, cond_recv, 1, left)
    acc_r = remote(xout.at[1], xin.at[0], acc_send, acc_recv, 0, right)
    acc_l = remote(xout.at[0], xin.at[1], acc_send, acc_recv, 1, left)

    def column(row8):
        return jnp.transpose(jnp.broadcast_to(row8[0:1, :], (TILE, TILE)))

    def hit(t, offset):
        at = jnp.maximum(t, 0)
        wanted = first_tile + at + offset
        found = jnp.int32(0)
        for s in range(nb_ref.shape[0]):
            same = jnp.logical_and(nb_ref[s, at] == wanted, s < cnt_ref[at])
            found = jnp.maximum(found, same.astype(jnp.int32))
        found = jnp.where(t >= 0, found, 0)
        return jnp.full((TILE, TILE), found, jnp.int32) > 0

    def paired(mask, value):
        return jnp.where(mask, value, 0.0)

    eye = lax.broadcasted_iota(jnp.int32, (TILE, TILE), 0) == lax.broadcasted_iota(
        jnp.int32, (TILE, TILE), 1
    )

    def part(slot, base, i, j):
        return gram[slot, base + i * TILE : base + (i + 1) * TILE, j * TILE : (j + 1) * TILE]

    def own_own(slot, base, k):
        e = 2 * k + LEAD
        near = hit(2 * k, 1)
        tiles_g = [[part(slot, base, i, j) for j in range(2)] for i in range(2)]
        rows_inv = []
        cols_inv = []
        for i in range(2):
            diag = jnp.sum(jnp.where(eye, tiles_g[i][i], 0.0), axis=0, keepdims=True)
            inv = jnp.broadcast_to(lax.rsqrt(diag + epsilon), (TILE, TILE))
            col = jnp.transpose(inv) * SCALE
            irow[e + i] = inv[0:8]
            icol[e + i] = col
            rows_inv.append(inv[0:1])
            cols_inv.append(col)
        cc = [column(crow[e]), column(crow[e + 1])]
        ccol[e] = cc[0]
        ccol[e + 1] = cc[1]
        w = [[None, None], [None, None]]
        for i in range(2):
            for j in range(2):
                v = jnp.exp2(tiles_g[i][j] * cols_inv[i] * rows_inv[j])
                w[i][j] = jnp.where(eye, 0.0, v) if i == j else paired(near, v)
        for j in range(2):
            acc[e + j, 0:8, :] = fold_rows(w[0][j] * cc[0] + w[1][j] * cc[1])
            acc[e + j, 8:16, :] = fold_rows(w[0][j] + w[1][j])

    def prev_own(slot, k):
        e = 2 * k + LEAD
        far0, near1, far1 = hit(2 * k - 2, 2), hit(2 * k - 1, 1), hit(2 * k - 1, 2)
        r0, r1 = irow[e, 0:1, :], irow[e + 1, 0:1, :]
        w00 = paired(far0, jnp.exp2(part(slot, 0, 0, 0) * icol[e - 2] * r0))
        w10 = paired(near1, jnp.exp2(part(slot, 0, 1, 0) * icol[e - 1] * r0))
        w11 = paired(far1, jnp.exp2(part(slot, 0, 1, 1) * icol[e - 1] * r1))
        cp0, cp1 = ccol[e - 2], ccol[e - 1]
        acc[e, 0:8, :] += fold_rows(w00 * cp0 + w10 * cp1)
        acc[e, 8:16, :] += fold_rows(w00 + w10)
        acc[e + 1, 0:8, :] += fold_rows(w11 * cp1)
        acc[e + 1, 8:16, :] += fold_rows(w11)
        c0, c1 = crow[e, 0:1, :], crow[e + 1, 0:1, :]
        acc[e - 2, 0:8, :] += fold_rows(jnp.transpose(w00 * c0))
        acc[e - 2, 8:16, :] += fold_rows(jnp.transpose(w00))
        acc[e - 1, 0:8, :] += fold_rows(jnp.transpose(w10 * c0 + w11 * c1))
        acc[e - 1, 8:16, :] += fold_rows(jnp.transpose(w10 + w11))

    def post(slot, k):
        own_own(slot, PAIR, k)
        prev_own(slot, k)

    def block(k, slot):
        start = pl.multiple_of(k * PAIR, PAIR)
        gram[slot] = gram_dot(own[pl.ds(start, 2 * PAIR), :], own[pl.ds(start + PAIR, PAIR), :])

    def send_halo():
        pl.semaphore_wait(barrier, devices - 1)

        @pl.when(has_right)
        def _():
            halo_r.start()
            cond_r.start()

        @pl.when(has_left)
        def _():
            halo_l.start()
            cond_l.start()

    @pl.when(jnp.logical_not(has_left))
    def _():
        halo[0:TILE, :] = jnp.zeros((TILE, species), halo.dtype)
        chalo[0] = jnp.zeros((8, TILE), jnp.float32)
        xin[0] = jnp.zeros((16, TILE), jnp.float32)

    @pl.when(jnp.logical_not(has_right))
    def _():
        halo[TILE:PAIR, :] = jnp.zeros((TILE, species), halo.dtype)
        chalo[1] = jnp.zeros((8, TILE), jnp.float32)
        xin[1] = jnp.zeros((16, TILE), jnp.float32)

    def step(i, carry):
        first = GROUP * i
        pl.when(i == HALO_AT)(send_halo)
        for u in range(GROUP):
            load(first + u).wait()
        for u in range(GROUP):
            block(first + u, u)
            post((u - 1) % GROUP, first + u - 1)
        return carry

    if HALO_AT < 0:
        send_halo()
    lax.fori_loop(0, pairs // GROUP, step, 0)
    @pl.when(has_left)
    def _():
        halo_r.wait_recv()
        cond_r.wait_recv()

    @pl.when(has_right)
    def _():
        halo_l.wait_recv()
        cond_l.wait_recv()

    def halo_inverse(side):
        total = jnp.zeros((TILE, TILE), jnp.float32)
        for q in range(species // TILE):
            x = halo[side * TILE : (side + 1) * TILE, q * TILE : (q + 1) * TILE]
            x = x.astype(jnp.float32)
            total = total + x * x
        inv = lax.rsqrt(jnp.sum(total, axis=1, keepdims=True) + epsilon)
        return jnp.transpose(jnp.broadcast_to(inv, (TILE, TILE)))

    post(GROUP - 1, pairs - 1)
    near_rows = jnp.concatenate(
        [own[PAIR : 2 * PAIR, :], own[rows : rows + TILE, :]], axis=0
    )
    edge = gram_dot(near_rows, halo[...])
    inv_l, inv_r = halo_inverse(0), halo_inverse(1)
    e0, e1, e22 = LEAD, LEAD + 1, LEAD + tiles - 2
    w0 = paired(hit(0, -1), jnp.exp2(edge[0:TILE, 0:TILE] * icol[e0] * inv_l))
    w1 = paired(hit(1, -2), jnp.exp2(edge[TILE:PAIR, 0:TILE] * icol[e1] * inv_l))
    w2 = paired(hit(tiles - 2, 2), jnp.exp2(edge[PAIR:, TILE:] * icol[e22] * inv_r))
    xout[0, 0:8, :] = fold_rows(w0 * ccol[e0] + w1 * ccol[e1])
    xout[0, 8:16, :] = fold_rows(w0 + w1)
    xout[1, 0:8, :] = fold_rows(w2 * ccol[e22])
    xout[1, 8:16, :] = fold_rows(w2)

    @pl.when(has_right)
    def _():
        acc_r.start()

    @pl.when(has_left)
    def _():
        acc_l.start()

    for e, w, side in ((e0, w0, 0), (e1, w1, 0), (e22, w2, 1)):
        acc[e, 0:8, :] += fold_rows(jnp.transpose(w * chalo[side, 0:1, :]))
        acc[e, 8:16, :] += fold_rows(jnp.transpose(w))

    line = lax.broadcasted_iota(jnp.int32, (16, TILE), 0)

    def finish(t, extra=None):
        e = t + LEAD
        total = acc[e]
        if extra is not None:
            total = total + xin[extra]
        numer = jnp.sum(total[0:8], axis=0, keepdims=True)
        denom = jnp.sum(total[8:16], axis=0, keepdims=True)
        eff = crow[e, 0:1, :] * numer / denom
        eff_ref[t : t + 1, :] = eff
        both = jnp.where(line == 0, eff, jnp.where(line == 1, 1.0, 0.0))
        wl[:, t * TILE : (t + 1) * TILE] = both.astype(jnp.bfloat16)

    for t in range(1, tiles - 1):
        finish(t)

    wide_step = 2048 if species % 2048 == 0 else TILE
    blocks = wide_step // TILE

    def inner(i, carry):
        cols = pl.ds(pl.multiple_of(i * wide_step, wide_step), wide_step)
        value = jnp.dot(
            wl[:, TILE : rows - TILE], own[PAIR + TILE : PAIR + rows - TILE, cols],
            preferred_element_type=jnp.float32,
        )
        for q in range(blocks):
            sums[i * blocks + q] = value[0:2, q * TILE : (q + 1) * TILE]
        return carry

    lax.fori_loop(0, species // wide_step, inner, 0)

    @pl.when(has_left)
    def _():
        acc_r.wait_recv()

    @pl.when(has_right)
    def _():
        acc_l.wait_recv()

    finish(0, 0)
    finish(tiles - 1, 1)

    eff_copy = pltpu.make_async_copy(eff_ref, eff_hbm, small_sem.at[0])
    eff_copy.start()
    share = wide // per

    chunks = species // wide_step

    def outer(i, carry):
        chunk = lax.rem(i + rank // (blocks * share) + chunks // 2, chunks)
        cols = pl.ds(pl.multiple_of(chunk * wide_step, wide_step), wide_step)
        ends = [own[PAIR : PAIR + TILE, cols], own[PAIR + rows - TILE : PAIR + rows, cols]]
        value = jnp.dot(
            jnp.concatenate([wl[:, 0:TILE], wl[:, rows - TILE : rows]], axis=1),
            jnp.concatenate(ends, axis=0), preferred_element_type=jnp.float32,
        )
        for q in range(blocks):
            sums[chunk * blocks + q] += value[0:2, q * TILE : (q + 1) * TILE]
        for q in range(blocks * share):
            owner = chunk * blocks * share + lax.rem(rank + q + blocks * share // 2, blocks * share)

            @pl.when(owner != rank)
            def _():
                pltpu.make_async_remote_copy(
                    src_ref=sums.at[owner // share],
                    dst_ref=got.at[lax.rem(rank - owner + devices, devices)],
                    send_sem=sum_send, recv_sem=sum_recv,
                    device_id=(owner // n_cell, lax.rem(owner, n_cell)), device_id_type=mesh_id,
                ).start()

        return carry

    lax.fori_loop(0, species // wide_step, outer, 0)
    got[0] = sums[rank // share]
    others = got.at[pl.ds(1, devices - 1)]
    pltpu.make_async_copy(others, others, sum_recv).wait()
    total = jnp.sum(got[...], axis=0)
    per_ref[...] = jnp.sqrt(jnp.sqrt(total[0:1, :] / total[1:2, :]))
    per_copy = pltpu.make_async_copy(per_ref, per_hbm, small_sem.at[1])
    per_copy.start()
    pltpu.make_async_copy(others, others, sum_send).wait()

    @pl.when(has_right)
    def _():
        halo_r.wait_send()
        cond_r.wait_send()
        acc_r.wait_send()

    @pl.when(has_left)
    def _():
        halo_l.wait_send()
        cond_l.wait_send()
        acc_l.wait_send()

    eff_copy.wait()
    per_copy.wait()


def close_kernel(eff_ref, per_ref, eff_out, per_out, sem):
    copies = [
        pltpu.make_async_copy(eff_ref, eff_out, sem.at[0]),
        pltpu.make_async_copy(per_ref, per_out, sem.at[1]),
    ]
    for copy in copies:
        copy.start()
    for copy in copies:
        copy.wait()


def per_device(n_grp, n_cell, occurrence, condition, neighbours, pair_count):
    tiles = pair_count.shape[0]
    rows, species = occurrence.shape
    devices = n_grp * n_cell
    per = species // devices
    wide = max(per, TILE)
    whole = pl.BlockSpec(memory_space=pl.ANY)
    dma = pltpu.SemaphoreType.DMA
    effective, persistence = pl.pallas_call(
        functools.partial(main_kernel, n_grp, n_cell, tiles, per, wide),
        out_shape=(
            jax.ShapeDtypeStruct((tiles, TILE), jnp.float32),
            jax.ShapeDtypeStruct((1, wide), jnp.float32),
        ),
        in_specs=[whole] * 4,
        out_specs=(whole, whole),
        scratch_shapes=[
            pltpu.VMEM((tiles, TILE), jnp.bfloat16),
            pltpu.SMEM((neighbours.shape[1], tiles), jnp.int32),
            pltpu.SMEM((tiles,), jnp.int32),
            pltpu.VMEM((tiles, TILE), jnp.float32),
            pltpu.VMEM((1, wide), jnp.float32),
            dma((3,)),
            pltpu.VMEM((PAIR + rows, species), jnp.bfloat16),
            pltpu.VMEM((PAIR, species), jnp.bfloat16),
            pltpu.VMEM((GROUP, 2 * PAIR, PAIR), jnp.float32),
            pltpu.VMEM((LEAD + tiles, 8, TILE), jnp.float32),
            pltpu.VMEM((LEAD + tiles, TILE, TILE), jnp.float32),
            pltpu.VMEM((LEAD + tiles, 8, TILE), jnp.float32),
            pltpu.VMEM((LEAD + tiles, TILE, TILE), jnp.float32),
            pltpu.VMEM((2, 8, TILE), jnp.float32),
            pltpu.VMEM((LEAD + tiles, 16, TILE), jnp.float32),
            pltpu.VMEM((2, 16, TILE), jnp.float32),
            pltpu.VMEM((2, 16, TILE), jnp.float32),
            pltpu.VMEM((16, rows), jnp.bfloat16),
            pltpu.VMEM((species // wide, 2, wide), jnp.float32),
            pltpu.VMEM((devices, 2, wide), jnp.float32),
            dma((tiles // 2,)), dma((2,)), dma((2,)), dma((2,)), dma((2,)), dma((2,)), dma((2,)),
            dma, dma,
        ],
        compiler_params=pltpu.CompilerParams(
            collective_id=0, has_side_effects=True, vmem_limit_bytes=56 * 2**20
        ),
    )(occurrence, condition.reshape(tiles, TILE), neighbours.T, pair_count)
    effective, persistence = pl.pallas_call(
        close_kernel,
        out_shape=(
            jax.ShapeDtypeStruct((tiles, TILE), jnp.float32),
            jax.ShapeDtypeStruct((1, wide), jnp.float32),
        ),
        in_specs=[whole] * 2,
        out_specs=(whole, whole),
        scratch_shapes=[dma((2,))],
    )(effective, persistence)
    persistence = persistence.reshape(wide)
    if per < wide:
        offset = lax.rem(lax.axis_index(("grp", "cell")) * per, wide)
        persistence = lax.dynamic_slice_in_dim(persistence, offset, per)
    return effective.reshape(rows), persistence


def solution(mesh):
    return jax.shard_map(
        functools.partial(per_device, mesh.shape["grp"], mesh.shape["cell"]),
        mesh=mesh,
        in_specs=(
            P(("grp", "cell"), None),
            P(("grp", "cell")),
            P(("grp", "cell"), None),
            P(("grp", "cell")),
        ),
        out_specs=(P(("grp", "cell")), P(("grp", "cell"))),
        check_vma=False,
    )
```

```python
import functools
import math

import jax
import jax.numpy as jnp
from jax import lax
from jax.experimental import pallas as pl
from jax.experimental.pallas import tpu as pltpu
from jax.sharding import PartitionSpec as P

sharpness = 40.0
epsilon = 1e-06

TILE = 128
PAIR = 2 * TILE
GROUP = 2
LEAD = 4
HALO_AT = 1
SCALE = sharpness * math.log2(math.e)


def gram_dot(a, b):
    return lax.dot_general(a, b, (((1,), (1,)), ((), ())), preferred_element_type=jnp.float32)


def fold_rows(x):
    return jnp.sum(x.reshape(x.shape[0] // 8, 8, x.shape[1]), axis=0)


def main_kernel(
    n_grp, n_cell, tiles, per, wide, occ_hbm, cond_hbm, nb_hbm, cnt_hbm, eff_ref, per_ref,
    cond_ref, nb_ref, cnt_ref, small_sem,
    own, halo, gram, irow, icol, crow, ccol, chalo, acc, xin, xout, wl, sums, got,
    load_sem, halo_send, halo_recv, cond_send, cond_recv, acc_send, acc_recv,
    sum_send, sum_recv,
):
    rows = tiles * TILE
    pairs = tiles // 2
    species = own.shape[1]
    devices = n_grp * n_cell
    grp = lax.axis_index("grp")
    me = lax.axis_index("cell")
    rank = grp * n_cell + me
    first_tile = rank * tiles
    has_left = me > 0
    has_right = me < n_cell - 1
    left = (grp, jnp.maximum(me - 1, 0))
    right = (grp, jnp.minimum(me + 1, n_cell - 1))
    mesh_id = pl.DeviceIdType.MESH

    def load(k):
        start = k * PAIR if isinstance(k, int) else pl.multiple_of(k * PAIR, PAIR)
        return pltpu.make_async_copy(
            occ_hbm.at[pl.ds(start, PAIR)], own.at[pl.ds(start + PAIR, PAIR)], load_sem.at[k]
        )

    barrier = pltpu.get_barrier_semaphore()

    small = [
        pltpu.make_async_copy(cond_hbm, cond_ref, small_sem.at[0]),
        pltpu.make_async_copy(nb_hbm, nb_ref, small_sem.at[1]),
        pltpu.make_async_copy(cnt_hbm, cnt_ref, small_sem.at[2]),
    ]
    for copy in small:
        copy.start()
    for k in range(2):
        load(k).start()

    def greet(j, carry):
        other = lax.rem(rank + j, devices)
        pl.semaphore_signal(
            barrier, inc=1, device_id=(other // n_cell, lax.rem(other, n_cell)),
            device_id_type=mesh_id,
        )
        return carry

    lax.fori_loop(1, devices, greet, 0, unroll=True)

    for k in range(2, pairs):
        load(k).start()
    for copy in small:
        copy.wait()

    cond = cond_ref[...].astype(jnp.float32)
    for e in range(LEAD):
        crow[e] = jnp.zeros((8, TILE), jnp.float32)
    for t in range(tiles):
        crow[t + LEAD] = jnp.broadcast_to(cond[t : t + 1, :], (8, TILE))

    def remote(src, dst, send, recv, slot, target):
        return pltpu.make_async_remote_copy(
            src_ref=src, dst_ref=dst, send_sem=send.at[slot], recv_sem=recv.at[slot],
            device_id=target, device_id_type=mesh_id,
        )

    halo_r = remote(
        occ_hbm.at[pl.ds(rows - TILE, TILE)], halo.at[pl.ds(0, TILE)], halo_send, halo_recv, 0, right
    )
    halo_l = remote(
        occ_hbm.at[pl.ds(0, TILE)], halo.at[pl.ds(TILE, TILE)], halo_send, halo_recv, 1, left
    )
    last = LEAD + tiles - 1
    cond_r = remote(crow.at[last], chalo.at[0], cond_send, cond_recv, 0, right)
    cond_l = remote(crow.at[LEAD], chalo.at[1], cond_send, cond_recv, 1, left)
    acc_r = remote(xout.at[1], xin.at[0], acc_send, acc_recv, 0, right)
    acc_l = remote(xout.at[0], xin.at[1], acc_send, acc_recv, 1, left)

    def column(row8):
        return jnp.transpose(jnp.broadcast_to(row8[0:1, :], (TILE, TILE)))

    def hit(t, offset):
        at = jnp.maximum(t, 0)
        wanted = first_tile + at + offset
        found = jnp.int32(0)
        for s in range(nb_ref.shape[0]):
            same = jnp.logical_and(nb_ref[s, at] == wanted, s < cnt_ref[at])
            found = jnp.maximum(found, same.astype(jnp.int32))
        found = jnp.where(t >= 0, found, 0)
        return jnp.full((TILE, TILE), found, jnp.int32) > 0

    def paired(mask, value):
        return jnp.where(mask, value, 0.0)

    eye = lax.broadcasted_iota(jnp.int32, (TILE, TILE), 0) == lax.broadcasted_iota(
        jnp.int32, (TILE, TILE), 1
    )

    def part(slot, base, i, j):
        return gram[slot, base + i * TILE : base + (i + 1) * TILE, j * TILE : (j + 1) * TILE]

    def own_own(slot, base, k):
        e = 2 * k + LEAD
        near = hit(2 * k, 1)
        tiles_g = [[part(slot, base, i, j) for j in range(2)] for i in range(2)]
        rows_inv = []
        cols_inv = []
        for i in range(2):
            diag = jnp.sum(jnp.where(eye, tiles_g[i][i], 0.0), axis=0, keepdims=True)
            inv = jnp.broadcast_to(lax.rsqrt(diag + epsilon), (TILE, TILE))
            col = jnp.transpose(inv) * SCALE
            irow[e + i] = inv[0:8]
            icol[e + i] = col
            rows_inv.append(inv[0:1])
            cols_inv.append(col)
        cc = [column(crow[e]), column(crow[e + 1])]
        ccol[e] = cc[0]
        ccol[e + 1] = cc[1]
        w = [[None, None], [None, None]]
        for i in range(2):
            for j in range(2):
                v = jnp.exp2(tiles_g[i][j] * cols_inv[i] * rows_inv[j])
                w[i][j] = jnp.where(eye, 0.0, v) if i == j else paired(near, v)
        for j in range(2):
            acc[e + j, 0:8, :] = fold_rows(w[0][j] * cc[0] + w[1][j] * cc[1])
            acc[e + j, 8:16, :] = fold_rows(w[0][j] + w[1][j])

    def prev_own(slot, k):
        e = 2 * k + LEAD
        far0, near1, far1 = hit(2 * k - 2, 2), hit(2 * k - 1, 1), hit(2 * k - 1, 2)
        r0, r1 = irow[e, 0:1, :], irow[e + 1, 0:1, :]
        w00 = paired(far0, jnp.exp2(part(slot, 0, 0, 0) * icol[e - 2] * r0))
        w10 = paired(near1, jnp.exp2(part(slot, 0, 1, 0) * icol[e - 1] * r0))
        w11 = paired(far1, jnp.exp2(part(slot, 0, 1, 1) * icol[e - 1] * r1))
        cp0, cp1 = ccol[e - 2], ccol[e - 1]
        acc[e, 0:8, :] += fold_rows(w00 * cp0 + w10 * cp1)
        acc[e, 8:16, :] += fold_rows(w00 + w10)
        acc[e + 1, 0:8, :] += fold_rows(w11 * cp1)
        acc[e + 1, 8:16, :] += fold_rows(w11)
        c0, c1 = crow[e, 0:1, :], crow[e + 1, 0:1, :]
        acc[e - 2, 0:8, :] += fold_rows(jnp.transpose(w00 * c0))
        acc[e - 2, 8:16, :] += fold_rows(jnp.transpose(w00))
        acc[e - 1, 0:8, :] += fold_rows(jnp.transpose(w10 * c0 + w11 * c1))
        acc[e - 1, 8:16, :] += fold_rows(jnp.transpose(w10 + w11))

    def post(slot, k):
        own_own(slot, PAIR, k)
        prev_own(slot, k)

    def block(k, slot):
        start = pl.multiple_of(k * PAIR, PAIR)
        gram[slot] = gram_dot(own[pl.ds(start, 2 * PAIR), :], own[pl.ds(start + PAIR, PAIR), :])

    def send_halo():
        pl.semaphore_wait(barrier, devices - 1)

        @pl.when(has_right)
        def _():
            halo_r.start()
            cond_r.start()

        @pl.when(has_left)
        def _():
            halo_l.start()
            cond_l.start()

    @pl.when(jnp.logical_not(has_left))
    def _():
        halo[0:TILE, :] = jnp.zeros((TILE, species), halo.dtype)
        chalo[0] = jnp.zeros((8, TILE), jnp.float32)
        xin[0] = jnp.zeros((16, TILE), jnp.float32)

    @pl.when(jnp.logical_not(has_right))
    def _():
        halo[TILE:PAIR, :] = jnp.zeros((TILE, species), halo.dtype)
        chalo[1] = jnp.zeros((8, TILE), jnp.float32)
        xin[1] = jnp.zeros((16, TILE), jnp.float32)

    def step(i, carry):
        first = GROUP * i
        pl.when(i == HALO_AT)(send_halo)
        for u in range(GROUP):
            load(first + u).wait()
        for u in range(GROUP):
            block(first + u, u)
            post((u - 1) % GROUP, first + u - 1)
        return carry

    if HALO_AT < 0:
        send_halo()
    lax.fori_loop(0, pairs // GROUP, step, 0)
    @pl.when(has_left)
    def _():
        halo_r.wait_recv()
        cond_r.wait_recv()

    @pl.when(has_right)
    def _():
        halo_l.wait_recv()
        cond_l.wait_recv()

    def halo_inverse(side):
        total = jnp.zeros((TILE, TILE), jnp.float32)
        for q in range(species // TILE):
            x = halo[side * TILE : (side + 1) * TILE, q * TILE : (q + 1) * TILE]
            x = x.astype(jnp.float32)
            total = total + x * x
        inv = lax.rsqrt(jnp.sum(total, axis=1, keepdims=True) + epsilon)
        return jnp.transpose(jnp.broadcast_to(inv, (TILE, TILE)))

    post(GROUP - 1, pairs - 1)
    near_rows = jnp.concatenate(
        [own[PAIR : 2 * PAIR, :], own[rows : rows + TILE, :]], axis=0
    )
    edge = gram_dot(near_rows, halo[...])
    inv_l, inv_r = halo_inverse(0), halo_inverse(1)
    e0, e1, e22 = LEAD, LEAD + 1, LEAD + tiles - 2
    w0 = paired(hit(0, -1), jnp.exp2(edge[0:TILE, 0:TILE] * icol[e0] * inv_l))
    w1 = paired(hit(1, -2), jnp.exp2(edge[TILE:PAIR, 0:TILE] * icol[e1] * inv_l))
    w2 = paired(hit(tiles - 2, 2), jnp.exp2(edge[PAIR:, TILE:] * icol[e22] * inv_r))
    xout[0, 0:8, :] = fold_rows(w0 * ccol[e0] + w1 * ccol[e1])
    xout[0, 8:16, :] = fold_rows(w0 + w1)
    xout[1, 0:8, :] = fold_rows(w2 * ccol[e22])
    xout[1, 8:16, :] = fold_rows(w2)

    @pl.when(has_right)
    def _():
        acc_r.start()

    @pl.when(has_left)
    def _():
        acc_l.start()

    for e, w, side in ((e0, w0, 0), (e1, w1, 0), (e22, w2, 1)):
        acc[e, 0:8, :] += fold_rows(jnp.transpose(w * chalo[side, 0:1, :]))
        acc[e, 8:16, :] += fold_rows(jnp.transpose(w))

    line = lax.broadcasted_iota(jnp.int32, (16, TILE), 0)

    def finish(t, extra=None):
        e = t + LEAD
        total = acc[e]
        if extra is not None:
            total = total + xin[extra]
        numer = jnp.sum(total[0:8], axis=0, keepdims=True)
        denom = jnp.sum(total[8:16], axis=0, keepdims=True)
        eff = crow[e, 0:1, :] * numer / denom
        eff_ref[t : t + 1, :] = eff
        both = jnp.where(line == 0, eff, jnp.where(line == 1, 1.0, 0.0))
        wl[:, t * TILE : (t + 1) * TILE] = both.astype(jnp.bfloat16)

    for t in range(1, tiles - 1):
        finish(t)

    wide_step = 2048 if species % 2048 == 0 else TILE
    blocks = wide_step // TILE

    def inner(i, carry):
        cols = pl.ds(pl.multiple_of(i * wide_step, wide_step), wide_step)
        value = jnp.dot(
            wl[:, TILE : rows - TILE], own[PAIR + TILE : PAIR + rows - TILE, cols],
            preferred_element_type=jnp.float32,
        )
        for q in range(blocks):
            sums[i * blocks + q] = value[0:2, q * TILE : (q + 1) * TILE]
        return carry

    lax.fori_loop(0, species // wide_step, inner, 0)

    @pl.when(has_left)
    def _():
        acc_r.wait_recv()

    @pl.when(has_right)
    def _():
        acc_l.wait_recv()

    finish(0, 0)
    finish(tiles - 1, 1)

    share = wide // per

    chunks = species // wide_step

    def outer(i, carry):
        chunk = lax.rem(i + rank // (blocks * share) + chunks // 2, chunks)
        cols = pl.ds(pl.multiple_of(chunk * wide_step, wide_step), wide_step)
        ends = [own[PAIR : PAIR + TILE, cols], own[PAIR + rows - TILE : PAIR + rows, cols]]
        value = jnp.dot(
            jnp.concatenate([wl[:, 0:TILE], wl[:, rows - TILE : rows]], axis=1),
            jnp.concatenate(ends, axis=0), preferred_element_type=jnp.float32,
        )
        for q in range(blocks):
            sums[chunk * blocks + q] += value[0:2, q * TILE : (q + 1) * TILE]
        for q in range(blocks * share):
            owner = chunk * blocks * share + lax.rem(rank + q + blocks * share // 2, blocks * share)

            @pl.when(owner != rank)
            def _():
                pltpu.make_async_remote_copy(
                    src_ref=sums.at[owner // share],
                    dst_ref=got.at[lax.rem(rank - owner + devices, devices)],
                    send_sem=sum_send, recv_sem=sum_recv,
                    device_id=(owner // n_cell, lax.rem(owner, n_cell)), device_id_type=mesh_id,
                ).start()

        return carry

    lax.fori_loop(0, species // wide_step, outer, 0)
    got[0] = sums[rank // share]
    others = got.at[pl.ds(1, devices - 1)]
    pltpu.make_async_copy(others, others, sum_recv).wait()
    total = jnp.sum(got[...], axis=0)
    per_ref[...] = jnp.sqrt(jnp.sqrt(total[0:1, :] / total[1:2, :]))
    pltpu.make_async_copy(others, others, sum_send).wait()

    @pl.when(has_right)
    def _():
        halo_r.wait_send()
        cond_r.wait_send()
        acc_r.wait_send()

    @pl.when(has_left)
    def _():
        halo_l.wait_send()
        cond_l.wait_send()
        acc_l.wait_send()


def per_device(n_grp, n_cell, occurrence, condition, neighbours, pair_count):
    tiles = pair_count.shape[0]
    rows, species = occurrence.shape
    devices = n_grp * n_cell
    per = species // devices
    wide = max(per, TILE)
    whole = pl.BlockSpec(memory_space=pl.ANY)
    vmem = pl.BlockSpec(memory_space=pltpu.VMEM)
    dma = pltpu.SemaphoreType.DMA
    effective, persistence = pl.pallas_call(
        functools.partial(main_kernel, n_grp, n_cell, tiles, per, wide),
        out_shape=(
            pltpu.VMEM((tiles, TILE), jnp.float32),
            pltpu.VMEM((1, wide), jnp.float32),
        ),
        in_specs=[whole] * 4,
        out_specs=(vmem, vmem),
        scratch_shapes=[
            pltpu.VMEM((tiles, TILE), jnp.bfloat16),
            pltpu.SMEM((neighbours.shape[1], tiles), jnp.int32),
            pltpu.SMEM((tiles,), jnp.int32),
            dma((3,)),
            pltpu.VMEM((PAIR + rows, species), jnp.bfloat16),
            pltpu.VMEM((PAIR, species), jnp.bfloat16),
            pltpu.VMEM((GROUP, 2 * PAIR, PAIR), jnp.float32),
            pltpu.VMEM((LEAD + tiles, 8, TILE), jnp.float32),
            pltpu.VMEM((LEAD + tiles, TILE, TILE), jnp.float32),
            pltpu.VMEM((LEAD + tiles, 8, TILE), jnp.float32),
            pltpu.VMEM((LEAD + tiles, TILE, TILE), jnp.float32),
            pltpu.VMEM((2, 8, TILE), jnp.float32),
            pltpu.VMEM((LEAD + tiles, 16, TILE), jnp.float32),
            pltpu.VMEM((2, 16, TILE), jnp.float32),
            pltpu.VMEM((2, 16, TILE), jnp.float32),
            pltpu.VMEM((16, rows), jnp.bfloat16),
            pltpu.VMEM((species // wide, 2, wide), jnp.float32),
            pltpu.VMEM((devices, 2, wide), jnp.float32),
            dma((tiles // 2,)), dma((2,)), dma((2,)), dma((2,)), dma((2,)), dma((2,)), dma((2,)),
            dma, dma,
        ],
        compiler_params=pltpu.CompilerParams(
            collective_id=0, has_side_effects=True, vmem_limit_bytes=56 * 2**20
        ),
    )(occurrence, condition.reshape(tiles, TILE), neighbours.T, pair_count)
    persistence = persistence.reshape(wide)
    if per < wide:
        offset = lax.rem(lax.axis_index(("grp", "cell")) * per, wide)
        persistence = lax.dynamic_slice_in_dim(persistence, offset, per)
    return effective.reshape(rows), persistence


def solution(mesh):
    return jax.shard_map(
        functools.partial(per_device, mesh.shape["grp"], mesh.shape["cell"]),
        mesh=mesh,
        in_specs=(
            P(("grp", "cell"), None),
            P(("grp", "cell")),
            P(("grp", "cell"), None),
            P(("grp", "cell")),
        ),
        out_specs=(P(("grp", "cell")), P(("grp", "cell"))),
        check_vma=False,
    )
```

```python
import functools
import math

import jax
import jax.numpy as jnp
from jax import lax
from jax.experimental import pallas as pl
from jax.experimental.pallas import tpu as pltpu
from jax.sharding import PartitionSpec as P

sharpness = 40.0
epsilon = 1e-06

TILE = 128
PAIR = 2 * TILE
GROUP = 2
LEAD = 4
SCALE = sharpness * math.log2(math.e)


def gram_dot(a, b):
    return lax.dot_general(a, b, (((1,), (1,)), ((), ())), preferred_element_type=jnp.float32)


def fold_rows(x):
    return jnp.sum(x.reshape(x.shape[0] // 8, 8, x.shape[1]), axis=0)


def main_kernel(
    n_grp, n_cell, tiles, per, wide, occ_hbm, cond_hbm, nb_hbm, cnt_hbm, eff_ref, per_ref,
    cond_ref, nb_ref, cnt_ref, small_sem,
    own, halo, gram, irow, icol, crow, ccol, chalo, acc, xin, xout, wl, sums, got,
    load_sem, halo_send, halo_recv, cond_send, cond_recv, acc_send, acc_recv,
    sum_send, sum_recv,
):
    rows = tiles * TILE
    pairs = tiles // 2
    species = own.shape[1]
    devices = n_grp * n_cell
    grp = lax.axis_index("grp")
    me = lax.axis_index("cell")
    rank = grp * n_cell + me
    first_tile = rank * tiles
    has_left = me > 0
    has_right = me < n_cell - 1
    left = (grp, jnp.maximum(me - 1, 0))
    right = (grp, jnp.minimum(me + 1, n_cell - 1))
    mesh_id = pl.DeviceIdType.MESH

    def load(k):
        start = k * PAIR if isinstance(k, int) else pl.multiple_of(k * PAIR, PAIR)
        return pltpu.make_async_copy(
            occ_hbm.at[pl.ds(start, PAIR)], own.at[pl.ds(start + PAIR, PAIR)], load_sem.at[k]
        )

    barrier = pltpu.get_barrier_semaphore()

    small = [
        pltpu.make_async_copy(cond_hbm, cond_ref, small_sem.at[0]),
        pltpu.make_async_copy(nb_hbm, nb_ref, small_sem.at[1]),
        pltpu.make_async_copy(cnt_hbm, cnt_ref, small_sem.at[2]),
    ]
    for copy in small:
        copy.start()
    for k in range(2):
        load(k).start()

    def greet(j, carry):
        other = lax.rem(rank + j, devices)
        pl.semaphore_signal(
            barrier, inc=1, device_id=(other // n_cell, lax.rem(other, n_cell)),
            device_id_type=mesh_id,
        )
        return carry

    lax.fori_loop(1, devices, greet, 0, unroll=True)

    for k in range(2, pairs):
        load(k).start()
    for copy in small:
        copy.wait()

    cond = cond_ref[...].astype(jnp.float32)
    for e in range(LEAD):
        crow[e] = jnp.zeros((8, TILE), jnp.float32)
    for t in range(tiles):
        crow[t + LEAD] = jnp.broadcast_to(cond[t : t + 1, :], (8, TILE))

    def remote(src, dst, send, recv, slot, target):
        return pltpu.make_async_remote_copy(
            src_ref=src, dst_ref=dst, send_sem=send.at[slot], recv_sem=recv.at[slot],
            device_id=target, device_id_type=mesh_id,
        )

    halo_r = remote(
        occ_hbm.at[pl.ds(rows - TILE, TILE)], halo.at[pl.ds(0, TILE)], halo_send, halo_recv, 0, right
    )
    halo_l = remote(
        occ_hbm.at[pl.ds(0, TILE)], halo.at[pl.ds(TILE, TILE)], halo_send, halo_recv, 1, left
    )
    last = LEAD + tiles - 1
    cond_r = remote(crow.at[last], chalo.at[0], cond_send, cond_recv, 0, right)
    cond_l = remote(crow.at[LEAD], chalo.at[1], cond_send, cond_recv, 1, left)
    acc_r = remote(xout.at[1], xin.at[0], acc_send, acc_recv, 0, right)
    acc_l = remote(xout.at[0], xin.at[1], acc_send, acc_recv, 1, left)

    def column(row8):
        return jnp.transpose(jnp.broadcast_to(row8[0:1, :], (TILE, TILE)))

    def hit(t, offset):
        at = jnp.maximum(t, 0)
        wanted = first_tile + at + offset
        found = jnp.int32(0)
        for s in range(nb_ref.shape[0]):
            same = jnp.logical_and(nb_ref[s, at] == wanted, s < cnt_ref[at])
            found = jnp.maximum(found, same.astype(jnp.int32))
        found = jnp.where(t >= 0, found, 0)
        return jnp.full((TILE, TILE), found, jnp.int32) > 0

    def paired(mask, value):
        return jnp.where(mask, value, 0.0)

    eye = lax.broadcasted_iota(jnp.int32, (TILE, TILE), 0) == lax.broadcasted_iota(
        jnp.int32, (TILE, TILE), 1
    )

    def part(slot, base, i, j):
        return gram[slot, base + i * TILE : base + (i + 1) * TILE, j * TILE : (j + 1) * TILE]

    def own_own(slot, base, k):
        e = 2 * k + LEAD
        near = hit(2 * k, 1)
        tiles_g = [[part(slot, base, i, j) for j in range(2)] for i in range(2)]
        rows_inv = []
        cols_inv = []
        for i in range(2):
            diag = jnp.sum(jnp.where(eye, tiles_g[i][i], 0.0), axis=0, keepdims=True)
            inv = jnp.broadcast_to(lax.rsqrt(diag + epsilon), (TILE, TILE))
            col = jnp.transpose(inv) * SCALE
            irow[e + i] = inv[0:8]
            icol[e + i] = col
            rows_inv.append(inv[0:1])
            cols_inv.append(col)
        cc = [column(crow[e]), column(crow[e + 1])]
        ccol[e] = cc[0]
        ccol[e + 1] = cc[1]
        w = [[None, None], [None, None]]
        for i in range(2):
            for j in range(2):
                v = jnp.exp2(tiles_g[i][j] * cols_inv[i] * rows_inv[j])
                w[i][j] = jnp.where(eye, 0.0, v) if i == j else paired(near, v)
        for j in range(2):
            acc[e + j, 0:8, :] = fold_rows(w[0][j] * cc[0] + w[1][j] * cc[1])
            acc[e + j, 8:16, :] = fold_rows(w[0][j] + w[1][j])

    def prev_own(slot, k):
        e = 2 * k + LEAD
        far0, near1, far1 = hit(2 * k - 2, 2), hit(2 * k - 1, 1), hit(2 * k - 1, 2)
        r0, r1 = irow[e, 0:1, :], irow[e + 1, 0:1, :]
        w00 = paired(far0, jnp.exp2(part(slot, 0, 0, 0) * icol[e - 2] * r0))
        w10 = paired(near1, jnp.exp2(part(slot, 0, 1, 0) * icol[e - 1] * r0))
        w11 = paired(far1, jnp.exp2(part(slot, 0, 1, 1) * icol[e - 1] * r1))
        cp0, cp1 = ccol[e - 2], ccol[e - 1]
        acc[e, 0:8, :] += fold_rows(w00 * cp0 + w10 * cp1)
        acc[e, 8:16, :] += fold_rows(w00 + w10)
        acc[e + 1, 0:8, :] += fold_rows(w11 * cp1)
        acc[e + 1, 8:16, :] += fold_rows(w11)
        c0, c1 = crow[e, 0:1, :], crow[e + 1, 0:1, :]
        acc[e - 2, 0:8, :] += fold_rows(jnp.transpose(w00 * c0))
        acc[e - 2, 8:16, :] += fold_rows(jnp.transpose(w00))
        acc[e - 1, 0:8, :] += fold_rows(jnp.transpose(w10 * c0 + w11 * c1))
        acc[e - 1, 8:16, :] += fold_rows(jnp.transpose(w10 + w11))

    def post(slot, k):
        own_own(slot, PAIR, k)
        prev_own(slot, k)

    def block(k, slot):
        start = k * PAIR if isinstance(k, int) else pl.multiple_of(k * PAIR, PAIR)
        gram[slot] = gram_dot(own[pl.ds(start, 2 * PAIR), :], own[pl.ds(start + PAIR, PAIR), :])

    def send_halo():
        pl.semaphore_wait(barrier, devices - 1)

        @pl.when(has_right)
        def _():
            halo_r.start()
            cond_r.start()

        @pl.when(has_left)
        def _():
            halo_l.start()
            cond_l.start()

    @pl.when(jnp.logical_not(has_left))
    def _():
        halo[0:TILE, :] = jnp.zeros((TILE, species), halo.dtype)
        chalo[0] = jnp.zeros((8, TILE), jnp.float32)
        xin[0] = jnp.zeros((16, TILE), jnp.float32)

    @pl.when(jnp.logical_not(has_right))
    def _():
        halo[TILE:PAIR, :] = jnp.zeros((TILE, species), halo.dtype)
        chalo[1] = jnp.zeros((8, TILE), jnp.float32)
        xin[1] = jnp.zeros((16, TILE), jnp.float32)

    def step(i, carry):
        first = 2 + GROUP * i
        for u in range(GROUP):
            load(first + u).wait()
        for u in range(GROUP):
            block(first + u, u)
            post((u - 1) % GROUP, first + u - 1)
        return carry

    load(0).wait()
    gram[0, PAIR:, :] = gram_dot(own[PAIR : 2 * PAIR, :], own[PAIR : 2 * PAIR, :])
    send_halo()
    load(1).wait()
    block(1, 1)
    own_own(0, PAIR, 0)
    lax.fori_loop(0, (pairs - 2) // GROUP, step, 0)
    @pl.when(has_left)
    def _():
        halo_r.wait_recv()
        cond_r.wait_recv()

    @pl.when(has_right)
    def _():
        halo_l.wait_recv()
        cond_l.wait_recv()

    def halo_inverse(side):
        total = jnp.zeros((TILE, TILE), jnp.float32)
        for q in range(species // TILE):
            x = halo[side * TILE : (side + 1) * TILE, q * TILE : (q + 1) * TILE]
            x = x.astype(jnp.float32)
            total = total + x * x
        inv = lax.rsqrt(jnp.sum(total, axis=1, keepdims=True) + epsilon)
        return jnp.transpose(jnp.broadcast_to(inv, (TILE, TILE)))

    post(GROUP - 1, pairs - 1)
    near_rows = jnp.concatenate(
        [own[PAIR : 2 * PAIR, :], own[rows : rows + TILE, :]], axis=0
    )
    edge = gram_dot(near_rows, halo[...])
    inv_l, inv_r = halo_inverse(0), halo_inverse(1)
    e0, e1, e22 = LEAD, LEAD + 1, LEAD + tiles - 2
    w0 = paired(hit(0, -1), jnp.exp2(edge[0:TILE, 0:TILE] * icol[e0] * inv_l))
    w1 = paired(hit(1, -2), jnp.exp2(edge[TILE:PAIR, 0:TILE] * icol[e1] * inv_l))
    w2 = paired(hit(tiles - 2, 2), jnp.exp2(edge[PAIR:, TILE:] * icol[e22] * inv_r))
    xout[0, 0:8, :] = fold_rows(w0 * ccol[e0] + w1 * ccol[e1])
    xout[0, 8:16, :] = fold_rows(w0 + w1)
    xout[1, 0:8, :] = fold_rows(w2 * ccol[e22])
    xout[1, 8:16, :] = fold_rows(w2)

    @pl.when(has_right)
    def _():
        acc_r.start()

    @pl.when(has_left)
    def _():
        acc_l.start()

    for e, w, side in ((e0, w0, 0), (e1, w1, 0), (e22, w2, 1)):
        acc[e, 0:8, :] += fold_rows(jnp.transpose(w * chalo[side, 0:1, :]))
        acc[e, 8:16, :] += fold_rows(jnp.transpose(w))

    line = lax.broadcasted_iota(jnp.int32, (16, TILE), 0)

    def finish(t, extra=None):
        e = t + LEAD
        total = acc[e]
        if extra is not None:
            total = total + xin[extra]
        numer = jnp.sum(total[0:8], axis=0, keepdims=True)
        denom = jnp.sum(total[8:16], axis=0, keepdims=True)
        eff = crow[e, 0:1, :] * numer / denom
        eff_ref[t : t + 1, :] = eff
        both = jnp.where(line == 0, eff, jnp.where(line == 1, 1.0, 0.0))
        wl[:, t * TILE : (t + 1) * TILE] = both.astype(jnp.bfloat16)

    for t in range(1, tiles - 1):
        finish(t)

    wide_step = 2048 if species % 2048 == 0 else TILE
    blocks = wide_step // TILE

    def inner(i, carry):
        cols = pl.ds(pl.multiple_of(i * wide_step, wide_step), wide_step)
        value = jnp.dot(
            wl[:, TILE : rows - TILE], own[PAIR + TILE : PAIR + rows - TILE, cols],
            preferred_element_type=jnp.float32,
        )
        for q in range(blocks):
            sums[i * blocks + q] = value[0:2, q * TILE : (q + 1) * TILE]
        return carry

    lax.fori_loop(0, species // wide_step, inner, 0)

    @pl.when(has_left)
    def _():
        acc_r.wait_recv()

    @pl.when(has_right)
    def _():
        acc_l.wait_recv()

    finish(0, 0)
    finish(tiles - 1, 1)

    share = wide // per

    chunks = species // wide_step

    def outer(i, carry):
        chunk = lax.rem(i + rank // (blocks * share) + chunks // 2, chunks)
        cols = pl.ds(pl.multiple_of(chunk * wide_step, wide_step), wide_step)
        ends = [own[PAIR : PAIR + TILE, cols], own[PAIR + rows - TILE : PAIR + rows, cols]]
        value = jnp.dot(
            jnp.concatenate([wl[:, 0:TILE], wl[:, rows - TILE : rows]], axis=1),
            jnp.concatenate(ends, axis=0), preferred_element_type=jnp.float32,
        )
        for q in range(blocks):
            sums[chunk * blocks + q] += value[0:2, q * TILE : (q + 1) * TILE]
        for q in range(blocks * share):
            owner = chunk * blocks * share + lax.rem(rank + q + blocks * share // 2, blocks * share)

            @pl.when(owner != rank)
            def _():
                pltpu.make_async_remote_copy(
                    src_ref=sums.at[owner // share],
                    dst_ref=got.at[lax.rem(rank - owner + devices, devices)],
                    send_sem=sum_send, recv_sem=sum_recv,
                    device_id=(owner // n_cell, lax.rem(owner, n_cell)), device_id_type=mesh_id,
                ).start()

        return carry

    lax.fori_loop(0, species // wide_step, outer, 0)
    got[0] = sums[rank // share]
    others = got.at[pl.ds(1, devices - 1)]
    pltpu.make_async_copy(others, others, sum_recv).wait()
    total = jnp.sum(got[...], axis=0)
    per_ref[...] = jnp.sqrt(jnp.sqrt(total[0:1, :] / total[1:2, :]))
    pltpu.make_async_copy(others, others, sum_send).wait()

    @pl.when(has_right)
    def _():
        halo_r.wait_send()
        cond_r.wait_send()
        acc_r.wait_send()

    @pl.when(has_left)
    def _():
        halo_l.wait_send()
        cond_l.wait_send()
        acc_l.wait_send()


def per_device(n_grp, n_cell, occurrence, condition, neighbours, pair_count):
    tiles = pair_count.shape[0]
    rows, species = occurrence.shape
    devices = n_grp * n_cell
    per = species // devices
    wide = max(per, TILE)
    whole = pl.BlockSpec(memory_space=pl.ANY)
    vmem = pl.BlockSpec(memory_space=pltpu.VMEM)
    dma = pltpu.SemaphoreType.DMA
    effective, persistence = pl.pallas_call(
        functools.partial(main_kernel, n_grp, n_cell, tiles, per, wide),
        out_shape=(
            pltpu.VMEM((tiles, TILE), jnp.float32),
            pltpu.VMEM((1, wide), jnp.float32),
        ),
        in_specs=[whole] * 4,
        out_specs=(vmem, vmem),
        scratch_shapes=[
            pltpu.VMEM((tiles, TILE), jnp.bfloat16),
            pltpu.SMEM((neighbours.shape[1], tiles), jnp.int32),
            pltpu.SMEM((tiles,), jnp.int32),
            dma((3,)),
            pltpu.VMEM((PAIR + rows, species), jnp.bfloat16),
            pltpu.VMEM((PAIR, species), jnp.bfloat16),
            pltpu.VMEM((GROUP, 2 * PAIR, PAIR), jnp.float32),
            pltpu.VMEM((LEAD + tiles, 8, TILE), jnp.float32),
            pltpu.VMEM((LEAD + tiles, TILE, TILE), jnp.float32),
            pltpu.VMEM((LEAD + tiles, 8, TILE), jnp.float32),
            pltpu.VMEM((LEAD + tiles, TILE, TILE), jnp.float32),
            pltpu.VMEM((2, 8, TILE), jnp.float32),
            pltpu.VMEM((LEAD + tiles, 16, TILE), jnp.float32),
            pltpu.VMEM((2, 16, TILE), jnp.float32),
            pltpu.VMEM((2, 16, TILE), jnp.float32),
            pltpu.VMEM((16, rows), jnp.bfloat16),
            pltpu.VMEM((species // wide, 2, wide), jnp.float32),
            pltpu.VMEM((devices, 2, wide), jnp.float32),
            dma((tiles // 2,)), dma((2,)), dma((2,)), dma((2,)), dma((2,)), dma((2,)), dma((2,)),
            dma, dma,
        ],
        compiler_params=pltpu.CompilerParams(
            collective_id=0, has_side_effects=True, vmem_limit_bytes=56 * 2**20
        ),
    )(occurrence, condition.reshape(tiles, TILE), neighbours.T, pair_count)
    persistence = persistence.reshape(wide)
    if per < wide:
        offset = lax.rem(lax.axis_index(("grp", "cell")) * per, wide)
        persistence = lax.dynamic_slice_in_dim(persistence, offset, per)
    return effective.reshape(rows), persistence


def solution(mesh):
    return jax.shard_map(
        functools.partial(per_device, mesh.shape["grp"], mesh.shape["cell"]),
        mesh=mesh,
        in_specs=(
            P(("grp", "cell"), None),
            P(("grp", "cell")),
            P(("grp", "cell"), None),
            P(("grp", "cell")),
        ),
        out_specs=(P(("grp", "cell")), P(("grp", "cell"))),
        check_vma=False,
    )
```

```python
import functools
import math

import jax
import jax.numpy as jnp
from jax import lax
from jax.experimental import pallas as pl
from jax.experimental.pallas import tpu as pltpu
from jax.sharding import PartitionSpec as P

sharpness = 40.0
epsilon = 1e-06

TILE = 128
PAIR = 2 * TILE
GROUP = 2
LEAD = 4
SCALE = sharpness * math.log2(math.e)


def gram_dot(a, b):
    return lax.dot_general(a, b, (((1,), (1,)), ((), ())), preferred_element_type=jnp.float32)


def fold_rows(x):
    return jnp.sum(x.reshape(x.shape[0] // 8, 8, x.shape[1]), axis=0)


def main_kernel(
    n_grp, n_cell, tiles, per, wide, occ_hbm, cond_ref, nb_hbm, cnt_hbm, eff_ref, per_ref,
    nb_ref, cnt_ref, small_sem,
    own, halo, gram, irow, icol, crow, ccol, chalo, acc, xin, xout, wl, sums, got,
    load_sem, halo_send, halo_recv, cond_send, cond_recv, acc_send, acc_recv,
    sum_send, sum_recv,
):
    rows = tiles * TILE
    pairs = tiles // 2
    species = own.shape[1]
    devices = n_grp * n_cell
    grp = lax.axis_index("grp")
    me = lax.axis_index("cell")
    rank = grp * n_cell + me
    first_tile = rank * tiles
    has_left = me > 0
    has_right = me < n_cell - 1
    left = (grp, jnp.maximum(me - 1, 0))
    right = (grp, jnp.minimum(me + 1, n_cell - 1))
    mesh_id = pl.DeviceIdType.MESH

    def load(k):
        start = k * PAIR if isinstance(k, int) else pl.multiple_of(k * PAIR, PAIR)
        return pltpu.make_async_copy(
            occ_hbm.at[pl.ds(start, PAIR)], own.at[pl.ds(start + PAIR, PAIR)], load_sem.at[k]
        )

    barrier = pltpu.get_barrier_semaphore()

    small = [
        pltpu.make_async_copy(nb_hbm, nb_ref, small_sem.at[1]),
        pltpu.make_async_copy(cnt_hbm, cnt_ref, small_sem.at[2]),
    ]
    for copy in small:
        copy.start()
    for k in range(2):
        load(k).start()

    def greet(j, carry):
        other = lax.rem(rank + j, devices)
        pl.semaphore_signal(
            barrier, inc=1, device_id=(other // n_cell, lax.rem(other, n_cell)),
            device_id_type=mesh_id,
        )
        return carry

    lax.fori_loop(1, devices, greet, 0, unroll=True)

    for k in range(2, pairs):
        load(k).start()
    for copy in small:
        copy.wait()

    cond = cond_ref[...].astype(jnp.float32)
    for e in range(LEAD):
        crow[e] = jnp.zeros((8, TILE), jnp.float32)
    for t in range(tiles):
        crow[t + LEAD] = jnp.broadcast_to(cond[t : t + 1, :], (8, TILE))

    def remote(src, dst, send, recv, slot, target):
        return pltpu.make_async_remote_copy(
            src_ref=src, dst_ref=dst, send_sem=send.at[slot], recv_sem=recv.at[slot],
            device_id=target, device_id_type=mesh_id,
        )

    halo_r = remote(
        occ_hbm.at[pl.ds(rows - TILE, TILE)], halo.at[pl.ds(0, TILE)], halo_send, halo_recv, 0, right
    )
    halo_l = remote(
        occ_hbm.at[pl.ds(0, TILE)], halo.at[pl.ds(TILE, TILE)], halo_send, halo_recv, 1, left
    )
    last = LEAD + tiles - 1
    cond_r = remote(crow.at[last], chalo.at[0], cond_send, cond_recv, 0, right)
    cond_l = remote(crow.at[LEAD], chalo.at[1], cond_send, cond_recv, 1, left)
    acc_r = remote(xout.at[1], xin.at[0], acc_send, acc_recv, 0, right)
    acc_l = remote(xout.at[0], xin.at[1], acc_send, acc_recv, 1, left)

    def column(row8):
        return jnp.transpose(jnp.broadcast_to(row8[0:1, :], (TILE, TILE)))

    def hit(t, offset):
        at = jnp.maximum(t, 0)
        wanted = first_tile + at + offset
        found = jnp.int32(0)
        for s in range(nb_ref.shape[0]):
            same = jnp.logical_and(nb_ref[s, at] == wanted, s < cnt_ref[at])
            found = jnp.maximum(found, same.astype(jnp.int32))
        found = jnp.where(t >= 0, found, 0)
        return jnp.full((TILE, TILE), found, jnp.int32) > 0

    def paired(mask, value):
        return jnp.where(mask, value, 0.0)

    eye = lax.broadcasted_iota(jnp.int32, (TILE, TILE), 0) == lax.broadcasted_iota(
        jnp.int32, (TILE, TILE), 1
    )

    def part(slot, base, i, j):
        return gram[slot, base + i * TILE : base + (i + 1) * TILE, j * TILE : (j + 1) * TILE]

    def own_own(slot, base, k):
        e = 2 * k + LEAD
        near = hit(2 * k, 1)
        tiles_g = [[part(slot, base, i, j) for j in range(2)] for i in range(2)]
        rows_inv = []
        cols_inv = []
        for i in range(2):
            diag = jnp.sum(jnp.where(eye, tiles_g[i][i], 0.0), axis=0, keepdims=True)
            inv = jnp.broadcast_to(lax.rsqrt(diag + epsilon), (TILE, TILE))
            col = jnp.transpose(inv) * SCALE
            irow[e + i] = inv[0:8]
            icol[e + i] = col
            rows_inv.append(inv[0:1])
            cols_inv.append(col)
        cc = [column(crow[e]), column(crow[e + 1])]
        ccol[e] = cc[0]
        ccol[e + 1] = cc[1]
        w = [[None, None], [None, None]]
        for i in range(2):
            for j in range(2):
                v = jnp.exp2(tiles_g[i][j] * cols_inv[i] * rows_inv[j])
                w[i][j] = jnp.where(eye, 0.0, v) if i == j else paired(near, v)
        for j in range(2):
            acc[e + j, 0:8, :] = fold_rows(w[0][j] * cc[0] + w[1][j] * cc[1])
            acc[e + j, 8:16, :] = fold_rows(w[0][j] + w[1][j])

    def prev_own(slot, k):
        e = 2 * k + LEAD
        far0, near1, far1 = hit(2 * k - 2, 2), hit(2 * k - 1, 1), hit(2 * k - 1, 2)
        r0, r1 = irow[e, 0:1, :], irow[e + 1, 0:1, :]
        w00 = paired(far0, jnp.exp2(part(slot, 0, 0, 0) * icol[e - 2] * r0))
        w10 = paired(near1, jnp.exp2(part(slot, 0, 1, 0) * icol[e - 1] * r0))
        w11 = paired(far1, jnp.exp2(part(slot, 0, 1, 1) * icol[e - 1] * r1))
        cp0, cp1 = ccol[e - 2], ccol[e - 1]
        acc[e, 0:8, :] += fold_rows(w00 * cp0 + w10 * cp1)
        acc[e, 8:16, :] += fold_rows(w00 + w10)
        acc[e + 1, 0:8, :] += fold_rows(w11 * cp1)
        acc[e + 1, 8:16, :] += fold_rows(w11)
        c0, c1 = crow[e, 0:1, :], crow[e + 1, 0:1, :]
        acc[e - 2, 0:8, :] += fold_rows(jnp.transpose(w00 * c0))
        acc[e - 2, 8:16, :] += fold_rows(jnp.transpose(w00))
        acc[e - 1, 0:8, :] += fold_rows(jnp.transpose(w10 * c0 + w11 * c1))
        acc[e - 1, 8:16, :] += fold_rows(jnp.transpose(w10 + w11))

    def post(slot, k):
        own_own(slot, PAIR, k)
        prev_own(slot, k)

    def block(k, slot):
        start = k * PAIR if isinstance(k, int) else pl.multiple_of(k * PAIR, PAIR)
        gram[slot] = gram_dot(own[pl.ds(start, 2 * PAIR), :], own[pl.ds(start + PAIR, PAIR), :])

    def send_halo():
        pl.semaphore_wait(barrier, devices - 1)

        @pl.when(has_right)
        def _():
            halo_r.start()
            cond_r.start()

        @pl.when(has_left)
        def _():
            halo_l.start()
            cond_l.start()

    @pl.when(jnp.logical_not(has_left))
    def _():
        halo[0:TILE, :] = jnp.zeros((TILE, species), halo.dtype)
        chalo[0] = jnp.zeros((8, TILE), jnp.float32)
        xin[0] = jnp.zeros((16, TILE), jnp.float32)

    @pl.when(jnp.logical_not(has_right))
    def _():
        halo[TILE:PAIR, :] = jnp.zeros((TILE, species), halo.dtype)
        chalo[1] = jnp.zeros((8, TILE), jnp.float32)
        xin[1] = jnp.zeros((16, TILE), jnp.float32)

    def step(i, carry):
        first = 2 + GROUP * i
        for u in range(GROUP):
            load(first + u).wait()
        for u in range(GROUP):
            block(first + u, u)
            post((u - 1) % GROUP, first + u - 1)
        return carry

    load(0).wait()
    gram[0, PAIR:, :] = gram_dot(own[PAIR : 2 * PAIR, :], own[PAIR : 2 * PAIR, :])
    send_halo()
    load(1).wait()
    block(1, 1)
    own_own(0, PAIR, 0)
    lax.fori_loop(0, (pairs - 2) // GROUP, step, 0)
    @pl.when(has_left)
    def _():
        halo_r.wait_recv()
        cond_r.wait_recv()

    @pl.when(has_right)
    def _():
        halo_l.wait_recv()
        cond_l.wait_recv()

    def halo_inverse(side):
        total = jnp.zeros((TILE, TILE), jnp.float32)
        for q in range(species // TILE):
            x = halo[side * TILE : (side + 1) * TILE, q * TILE : (q + 1) * TILE]
            x = x.astype(jnp.float32)
            total = total + x * x
        inv = lax.rsqrt(jnp.sum(total, axis=1, keepdims=True) + epsilon)
        return jnp.transpose(jnp.broadcast_to(inv, (TILE, TILE)))

    post(GROUP - 1, pairs - 1)
    near_rows = jnp.concatenate(
        [own[PAIR : 2 * PAIR, :], own[rows : rows + TILE, :]], axis=0
    )
    edge = gram_dot(near_rows, halo[...])
    inv_l, inv_r = halo_inverse(0), halo_inverse(1)
    e0, e1, e22 = LEAD, LEAD + 1, LEAD + tiles - 2
    w0 = paired(hit(0, -1), jnp.exp2(edge[0:TILE, 0:TILE] * icol[e0] * inv_l))
    w1 = paired(hit(1, -2), jnp.exp2(edge[TILE:PAIR, 0:TILE] * icol[e1] * inv_l))
    w2 = paired(hit(tiles - 2, 2), jnp.exp2(edge[PAIR:, TILE:] * icol[e22] * inv_r))
    xout[0, 0:8, :] = fold_rows(w0 * ccol[e0] + w1 * ccol[e1])
    xout[0, 8:16, :] = fold_rows(w0 + w1)
    xout[1, 0:8, :] = fold_rows(w2 * ccol[e22])
    xout[1, 8:16, :] = fold_rows(w2)

    @pl.when(has_right)
    def _():
        acc_r.start()

    @pl.when(has_left)
    def _():
        acc_l.start()

    for e, w, side in ((e0, w0, 0), (e1, w1, 0), (e22, w2, 1)):
        acc[e, 0:8, :] += fold_rows(jnp.transpose(w * chalo[side, 0:1, :]))
        acc[e, 8:16, :] += fold_rows(jnp.transpose(w))

    line = lax.broadcasted_iota(jnp.int32, (16, TILE), 0)

    def finish(t, extra=None):
        e = t + LEAD
        total = acc[e]
        if extra is not None:
            total = total + xin[extra]
        numer = jnp.sum(total[0:8], axis=0, keepdims=True)
        denom = jnp.sum(total[8:16], axis=0, keepdims=True)
        eff = crow[e, 0:1, :] * numer / denom
        eff_ref[t : t + 1, :] = eff
        both = jnp.where(line == 0, eff, jnp.where(line == 1, 1.0, 0.0))
        wl[:, t * TILE : (t + 1) * TILE] = both.astype(jnp.bfloat16)

    for t in range(1, tiles - 1):
        finish(t)

    wide_step = 2048 if species % 2048 == 0 else TILE
    blocks = wide_step // TILE

    def inner(i, carry):
        cols = pl.ds(pl.multiple_of(i * wide_step, wide_step), wide_step)
        value = jnp.dot(
            wl[:, TILE : rows - TILE], own[PAIR + TILE : PAIR + rows - TILE, cols],
            preferred_element_type=jnp.float32,
        )
        for q in range(blocks):
            sums[i * blocks + q] = value[0:2, q * TILE : (q + 1) * TILE]
        return carry

    lax.fori_loop(0, species // wide_step, inner, 0)

    @pl.when(has_left)
    def _():
        acc_r.wait_recv()

    @pl.when(has_right)
    def _():
        acc_l.wait_recv()

    finish(0, 0)
    finish(tiles - 1, 1)

    share = wide // per

    chunks = species // wide_step

    def outer(i, carry):
        chunk = lax.rem(i + rank // (blocks * share) + chunks // 2, chunks)
        cols = pl.ds(pl.multiple_of(chunk * wide_step, wide_step), wide_step)
        ends = [own[PAIR : PAIR + TILE, cols], own[PAIR + rows - TILE : PAIR + rows, cols]]
        value = jnp.dot(
            jnp.concatenate([wl[:, 0:TILE], wl[:, rows - TILE : rows]], axis=1),
            jnp.concatenate(ends, axis=0), preferred_element_type=jnp.float32,
        )
        for q in range(blocks):
            sums[chunk * blocks + q] += value[0:2, q * TILE : (q + 1) * TILE]
        for q in range(blocks * share):
            owner = chunk * blocks * share + lax.rem(rank + q + blocks * share // 2, blocks * share)

            @pl.when(owner != rank)
            def _():
                pltpu.make_async_remote_copy(
                    src_ref=sums.at[owner // share],
                    dst_ref=got.at[lax.rem(rank - owner + devices, devices)],
                    send_sem=sum_send, recv_sem=sum_recv,
                    device_id=(owner // n_cell, lax.rem(owner, n_cell)), device_id_type=mesh_id,
                ).start()

        return carry

    lax.fori_loop(0, species // wide_step, outer, 0)
    got[0] = sums[rank // share]
    others = got.at[pl.ds(1, devices - 1)]
    pltpu.make_async_copy(others, others, sum_recv).wait()
    total = jnp.sum(got[...], axis=0)
    per_ref[...] = jnp.sqrt(jnp.sqrt(total[0:1, :] / total[1:2, :]))
    pltpu.make_async_copy(others, others, sum_send).wait()

    @pl.when(has_right)
    def _():
        halo_r.wait_send()
        cond_r.wait_send()
        acc_r.wait_send()

    @pl.when(has_left)
    def _():
        halo_l.wait_send()
        cond_l.wait_send()
        acc_l.wait_send()


def per_device(n_grp, n_cell, occurrence, condition, neighbours, pair_count):
    tiles = pair_count.shape[0]
    rows, species = occurrence.shape
    devices = n_grp * n_cell
    per = species // devices
    wide = max(per, TILE)
    whole = pl.BlockSpec(memory_space=pl.ANY)
    vmem = pl.BlockSpec(memory_space=pltpu.VMEM)
    dma = pltpu.SemaphoreType.DMA
    effective, persistence = pl.pallas_call(
        functools.partial(main_kernel, n_grp, n_cell, tiles, per, wide),
        out_shape=(
            pltpu.VMEM((tiles, TILE), jnp.float32),
            pltpu.VMEM((1, wide), jnp.float32),
        ),
        in_specs=[whole, vmem, whole, whole],
        out_specs=(vmem, vmem),
        scratch_shapes=[
            pltpu.SMEM((neighbours.shape[1], tiles), jnp.int32),
            pltpu.SMEM((tiles,), jnp.int32),
            dma((3,)),
            pltpu.VMEM((PAIR + rows, species), jnp.bfloat16),
            pltpu.VMEM((PAIR, species), jnp.bfloat16),
            pltpu.VMEM((GROUP, 2 * PAIR, PAIR), jnp.float32),
            pltpu.VMEM((LEAD + tiles, 8, TILE), jnp.float32),
            pltpu.VMEM((LEAD + tiles, TILE, TILE), jnp.float32),
            pltpu.VMEM((LEAD + tiles, 8, TILE), jnp.float32),
            pltpu.VMEM((LEAD + tiles, TILE, TILE), jnp.float32),
            pltpu.VMEM((2, 8, TILE), jnp.float32),
            pltpu.VMEM((LEAD + tiles, 16, TILE), jnp.float32),
            pltpu.VMEM((2, 16, TILE), jnp.float32),
            pltpu.VMEM((2, 16, TILE), jnp.float32),
            pltpu.VMEM((16, rows), jnp.bfloat16),
            pltpu.VMEM((species // wide, 2, wide), jnp.float32),
            pltpu.VMEM((devices, 2, wide), jnp.float32),
            dma((tiles // 2,)), dma((2,)), dma((2,)), dma((2,)), dma((2,)), dma((2,)), dma((2,)),
            dma, dma,
        ],
        compiler_params=pltpu.CompilerParams(
            collective_id=0, has_side_effects=True, vmem_limit_bytes=56 * 2**20
        ),
    )(occurrence, condition.reshape(tiles, TILE), neighbours.T, pair_count)
    persistence = persistence.reshape(wide)
    if per < wide:
        offset = lax.rem(lax.axis_index(("grp", "cell")) * per, wide)
        persistence = lax.dynamic_slice_in_dim(persistence, offset, per)
    return effective.reshape(rows), persistence


def solution(mesh):
    return jax.shard_map(
        functools.partial(per_device, mesh.shape["grp"], mesh.shape["cell"]),
        mesh=mesh,
        in_specs=(
            P(("grp", "cell"), None),
            P(("grp", "cell")),
            P(("grp", "cell"), None),
            P(("grp", "cell")),
        ),
        out_specs=(P(("grp", "cell")), P(("grp", "cell"))),
        check_vma=False,
    )
```
